128 devices in a mesh: fsdp: 16 (over z, y), tp: 2 (over core), rep: 4 (over x).
Axes of the slice: x: 4, y: 4, z: 4, core: 2. Of those that a mesh axis runs over, the one named last changes fastest.
Arguments:
- out_momentum: float32 [5120, 5120], P(('fsdp', 'rep'), 'tp'), may hold values from -80 to 80
- out_gradient: bfloat16 [5120, 5120], P(('fsdp', 'rep'), 'tp'), may hold values from -6 to 6
- out_weight: bfloat16 [5120, 5120], P(('fsdp', 'rep'), 'tp'), may hold values from -0.078125 to 0.078125
- out_right: float32 [5120, 128], P('tp'), may hold values from -0.078125 to 0.078125
- up_momentum: float32 [5120, 13824], P(('fsdp', 'rep'), 'tp'), may hold values from -80 to 80
- up_gradient: bfloat16 [5120, 13824], P(('fsdp', 'rep'), 'tp'), may hold values from -6 to 6
- up_weight: bfloat16 [5120, 13824], P(('fsdp', 'rep'), 'tp'), may hold values from -0.078125 to 0.078125
- up_right: float32 [13824, 128], P('tp'), may hold values from -0.0546875 to 0.0546875
- down_momentum: float32 [13824, 5120], P(('fsdp', 'rep'), 'tp'), may hold values from -80 to 80
- down_gradient: bfloat16 [13824, 5120], P(('fsdp', 'rep'), 'tp'), may hold values from -6 to 6
- down_weight: bfloat16 [13824, 5120], P(('fsdp', 'rep'), 'tp'), may hold values from -0.0546875 to 0.0546875
- down_right: float32 [5120, 128], P('tp'), may hold values from -0.078125 to 0.078125
Outputs:
- out_momentum_next: float32 [5120, 5120], P(('fsdp', 'rep'), 'tp')
- up_momentum_next: float32 [5120, 13824], P(('fsdp', 'rep'), 'tp')
- down_momentum_next: float32 [13824, 5120], P(('fsdp', 'rep'), 'tp')
- out_weight_next: bfloat16 [5120, 5120], P(('fsdp', 'rep'), 'tp')
- up_weight_next: bfloat16 [5120, 13824], P(('fsdp', 'rep'), 'tp')
- down_weight_next: bfloat16 [13824, 5120], P(('fsdp', 'rep'), 'tp')
- out_right_next: float32 [5120, 128], P('tp')
- up_right_next: float32 [13824, 128], P('tp')
- down_right_next: float32 [5120, 128], P('tp')
- out_update: float32 [5120, 5120], P(('fsdp', 'rep'), 'tp')
- up_update: float32 [5120, 13824], P(('fsdp', 'rep'), 'tp')
- down_update: float32 [13824, 5120], P(('fsdp', 'rep'), 'tp')
The draws below stay inside these ranges and needn't reach their ends.
All inputs are finite; a program needn't handle non-finite values.
Results may differ from the reference program's by a relative error of at most 0.001.
Values sent between devices are 32-bit elements; how exact they have to be, the bound alone decides.
A program may use at most 128 MiB of HBM per device.

```python
import math
import jax
import jax.numpy as jnp
from jax import lax

D = 5120
FF = 13824
RANK = 128


def scale_table(key, row_count, col_count):
    row_key, col_key = jax.random.split(key)
    position = jnp.arange(row_count, dtype=jnp.float32) / row_count
    row_scale = 0.5 * jnp.exp(jnp.log(3.0) * position + jax.random.uniform(row_key, (row_count,), jnp.float32, -1.1513, 1.1513))
    col_scale = jnp.exp(jax.random.uniform(col_key, (col_count,), jnp.float32, -1.1513, 1.1513))
    return row_scale[:, None] * col_scale[None, :]


def draw_out_momentum(key, part):
    key = jax.random.fold_in(key, 11)
    base_key, scale_key = jax.random.split(key, 2)
    scales = scale_table(scale_key, D, D)
    values = jnp.clip(jax.random.normal(base_key, (D, D), jnp.float32), -4.0, 4.0)
    return values * scales


def draw_up_momentum(key, part):
    key = jax.random.fold_in(key, 23)
    base_key, scale_key = jax.random.split(key, 2)
    scales = scale_table(scale_key, D, FF)
    values = jnp.clip(jax.random.normal(base_key, (D, FF), jnp.float32), -4.0, 4.0)
    return values * scales


def draw_down_momentum(key, part):
    key = jax.random.fold_in(key, 37)
    base_key, scale_key = jax.random.split(key, 2)
    scales = scale_table(scale_key, FF, D)
    values = jnp.clip(jax.random.normal(base_key, (FF, D), jnp.float32), -4.0, 4.0)
    return values * scales


def level_of(rng, extent, cuts, low, largest):
    level, own = 1.0, jax.random.fold_in(rng, 6)
    for dim, parts in cuts:
        draws = jnp.exp(jax.random.uniform(jax.random.fold_in(own, dim), (parts,), jnp.float32, low / len(cuts), largest / len(cuts)))
        level = level * jnp.repeat(draws, extent[dim] // parts).reshape([-1 if axis == dim else 1 for axis in range(len(extent))])
    return level


def bell_draw(rng, dims, deviation, bound, shards=(), kind=jnp.bfloat16):
    loudness = level_of(rng, dims, shards, -0.22, 0.18) if shards else 1.0
    values = jax.random.normal(rng, dims, jnp.float32) * deviation * loudness
    return jnp.minimum(jnp.maximum(values, -bound), bound).astype(kind)


def setup_inputs(seed: int = 0) -> dict:
    streams_of = jax.random.split(jax.random.key(seed), 13)
    out_momentum = draw_out_momentum(jax.random.fold_in(streams_of[12], 71), 0)
    out_gradient = bell_draw(streams_of[1], (D, D), 1.0, 6.0, ((0, 64), (1, 2)))
    out_weight = bell_draw(streams_of[2], (D, D), D ** -0.5, 0.078125, ((0, 64), (1, 2)))
    out_right = bell_draw(streams_of[3], (D, RANK), D ** -0.5, 0.078125, ((0, 2),), jnp.float32)
    up_momentum = draw_up_momentum(jax.random.fold_in(streams_of[12], 71), 0)
    up_gradient = bell_draw(streams_of[5], (D, FF), 1.0, 6.0, ((0, 64), (1, 2)))
    up_weight = bell_draw(streams_of[6], (D, FF), D ** -0.5, 0.078125, ((0, 64), (1, 2)))
    up_right = bell_draw(streams_of[7], (FF, RANK), FF ** -0.5, 0.0546875, ((0, 2),), jnp.float32)
    down_momentum = draw_down_momentum(jax.random.fold_in(streams_of[12], 71), 0)
    down_gradient = bell_draw(streams_of[9], (FF, D), 1.0, 6.0, ((0, 64), (1, 2)))
    down_weight = bell_draw(streams_of[10], (FF, D), FF ** -0.5, 0.0546875, ((0, 64), (1, 2)))
    down_right = bell_draw(streams_of[11], (D, RANK), D ** -0.5, 0.078125, ((0, 2),), jnp.float32)
    return {"out_momentum": out_momentum, "out_gradient": out_gradient, "out_weight": out_weight, "out_right": out_right, "up_momentum": up_momentum, "up_gradient": up_gradient, "up_weight": up_weight, "up_right": up_right, "down_momentum": down_momentum, "down_gradient": down_gradient, "down_weight": down_weight, "down_right": down_right}


DECAY = 0.95
LEARN_RATE = 0.02
EPSILON = 1e-08

def exact_dot(first, second):
    return jnp.dot(first, second, precision=lax.Precision.HIGHEST)

def dion_update(momentum, gradient, weight, right_factor):
    row_count, col_count = momentum.shape
    buffer = momentum + gradient.astype(jnp.float32)
    left_factor = exact_dot(buffer, right_factor)
    gram_matrix = exact_dot(left_factor.T, left_factor)
    lower_factor = jnp.linalg.cholesky(gram_matrix)
    identity = jnp.eye(gram_matrix.shape[0], dtype=jnp.float32)
    inverse = lax.linalg.triangular_solve(lower_factor, identity, left_side=True, lower=True)
    left_basis = exact_dot(left_factor, inverse.T)
    summed_factor = exact_dot(buffer.T, left_basis)
    momentum_next = buffer - (1.0 - DECAY) * exact_dot(left_basis, summed_factor.T)
    column_squares = lax.optimization_barrier(jnp.sum(summed_factor * summed_factor, axis=0))
    right_next = summed_factor / (jnp.sqrt(column_squares) + EPSILON)
    step_size = LEARN_RATE * math.sqrt(row_count / col_count)
    change = step_size * exact_dot(left_basis, right_next.T)
    weight_next = (weight.astype(jnp.float32) - change).astype(jnp.bfloat16)
    return (momentum_next, weight_next, right_next, change)

def reference(out_momentum, out_gradient, out_weight, out_right, up_momentum, up_gradient, up_weight, up_right, down_momentum, down_gradient, down_weight, down_right):
    out_moment, out_matrix, out_factor, out_change = dion_update(out_momentum, out_gradient, out_weight, out_right)
    up_moment, up_matrix, up_factor, up_change = dion_update(up_momentum, up_gradient, up_weight, up_right)
    down_moment, down_matrix, down_factor, down_change = dion_update(down_momentum, down_gradient, down_weight, down_right)
    return (out_moment, up_moment, down_moment, out_matrix, up_matrix, down_matrix, out_factor, up_factor, down_factor, out_change, up_change, down_change)
```

```python
import functools
import math

import jax
import jax.numpy as jnp
from jax import lax
from jax.experimental import pallas as pl
from jax.experimental.pallas import tpu as pltpu
from jax.sharding import PartitionSpec as P

ROWS = (216, 80, 80)
PADDED = (224, 80, 80)
COLS = (2560, 2560, 6912)
UNITS = (5, 5, 14)
SPANS = ((1280, 1280), (1280, 1280), (2304, 2304, 2304))
SHAPE = ((13824, 5120), (5120, 5120), (5120, 13824))
UNIT = 512
RANK = 128
DECAY = 0.95
LEARN_RATE = 0.02
EPSILON = 1e-08
MESH = pl.DeviceIdType.MESH
F32 = jnp.float32
BF16 = jnp.bfloat16
HIGHEST = lax.Precision.HIGHEST
AXES = ((0, 1, 2), (1, 2, 0), (2, 0, 1))
TERMS = tuple(3 * rows + (-3 * rows) % 128 for rows in PADDED)

PER_PART = (3, 5)


def make_parts():
    units = [(matrix, unit) for matrix in range(3) for unit in range(UNITS[matrix])]
    parts = []
    for count in PER_PART:
        for _ in range(3):
            parts.append(units[:count])
            units = units[count:]
    return parts


PARTS = make_parts()
N_PARTS = len(PARTS)
HEIGHT = [8 * len(part) for part in PARTS]


def split(value):
    high = value.astype(BF16)
    return high, (value - high.astype(F32)).astype(BF16)


def nt_dot(first, second, precision=None):
    return lax.dot_general(first, second, (((1,), (1,)), ((), ())), precision=precision, preferred_element_type=F32)


def tn_dot(first, second, precision=None):
    return lax.dot_general(first, second, (((0,), (0,)), ((), ())), precision=precision, preferred_element_type=F32)


def each(count, body):
    def step(index, carry):
        body(index)
        return carry

    lax.fori_loop(0, count, step, 0)


def reduce_kernel(
    momentum,
    gradient,
    right,
    factor,
    buffer,
    basis,
    squares,
    partial,
    summed,
    inbox1,
    inbox2,
    inbox3,
    grad_in,
    right_in,
    terms,
    right_terms,
    left,
    left_in,
    left_terms,
    gram,
    gram_in1,
    gram_in2,
    gram_in3,
    gram_sum,
    gram_all,
    matrix,
    inverse,
    squares_in,
    load_sem,
    send_sem,
    recv_sem,
    misc_send,
    misc_recv,
):
    rows_at = lax.axis_index("fsdp")
    core = lax.axis_index("tp")
    coord = (lax.axis_index("rep"), rows_at % 4, rows_at // 4)

    def device(axis, shift):
        moved = [(coord[a] + shift) % 4 if a == axis else coord[a] for a in range(3)]
        return (moved[2] * 4 + moved[1], core, moved[0])

    partner = (rows_at, 1 - core, coord[0])

    loads = []
    for j in range(3):
        steps = []
        start = 0
        for s, span in enumerate(SPANS[j]):
            cols = pl.ds(start, span)
            copies = [
                pltpu.make_async_copy(momentum[j].at[:, cols], buffer[j].at[:, cols], load_sem.at[j, s, 0]),
                pltpu.make_async_copy(gradient[j].at[:, cols], grad_in[j].at[:, cols], load_sem.at[j, s, 1]),
                pltpu.make_async_copy(right[j].at[cols, :], right_in[j].at[cols, :], load_sem.at[j, s, 2]),
            ]
            for copy in copies:
                copy.start()
            steps.append((start, span, copies))
            start += span
        loads.append(steps)

    barrier = pltpu.get_barrier_semaphore()
    peers = [device(axis, shift) for axis in range(3) for shift in (1, 2, 3)] + [partner]
    for peer in peers:
        pl.semaphore_signal(barrier, inc=1, device_id=peer, device_id_type=MESH)

    started = []

    def send(index, src, dst, target, sems=None):
        first, second = (send_sem, recv_sem) if sems is None else sems
        copy = pltpu.make_async_remote_copy(
            src_ref=src,
            dst_ref=dst,
            send_sem=first.at[index],
            recv_sem=second.at[index],
            device_id=target,
            device_id_type=MESH,
        )
        copy.start()
        started.append(copy)
        return copy

    misc = functools.partial(send, sems=(misc_send, misc_recv))

    def left_partial(j):
        pad = PADDED[j]
        total = None
        for start, span, copies in loads[j]:
            for copy in copies:
                copy.wait()

            def prepare(i, start=start):
                cols = pl.ds(pl.multiple_of(start + i * 256, 256), 256)
                value = buffer[j][:, cols] + grad_in[j][:, cols].astype(F32)
                buffer[j][:, cols] = value
                if pad > ROWS[j]:
                    value = jnp.concatenate([value, jnp.zeros((pad - ROWS[j], 256), F32)], axis=0)
                high, low = split(value)
                terms[j][0:pad, cols] = high
                terms[j][pad : 2 * pad, cols] = low
                terms[j][2 * pad : 3 * pad, cols] = high
                high, low = split(right_in[j][cols, :])
                right_terms[j][cols, 0:RANK] = high
                right_terms[j][cols, RANK : 2 * RANK] = low

            each(span // 256, prepare)
            product = jnp.dot(
                terms[j][0 : 2 * pad, start : start + span],
                right_terms[j][start : start + span, :],
                preferred_element_type=F32,
            )
            product = product[0:pad, 0:RANK] + (product[0:pad, RANK:] + product[pad:, 0:RANK])
            total = product if total is None else total + product
        left[j][...] = total
        if terms[j].shape[1] > COLS[j]:
            terms[j][:, COLS[j] :] = jnp.zeros((3 * pad, terms[j].shape[1] - COLS[j]), BF16)
        return misc(j, left[j], left_in[j], partner)

    def left_finish(j, copy):
        copy.wait_recv()
        pad = PADDED[j]
        value = left[j][...] + left_in[j][...]
        left_in[j][...] = value
        high = value.astype(BF16).astype(F32)
        low = value - high
        pieces = [high, high, low]
        if TERMS[j] > 3 * pad:
            pieces.append(jnp.zeros((TERMS[j] - 3 * pad, RANK), F32))
        left_terms[j][...] = jnp.concatenate(pieces, axis=0).T.astype(BF16)

    def gram_partial(j):
        value = left_in[j][...]
        result = tn_dot(value, value, HIGHEST)
        gram[:, :, j] = result.reshape(2, 4, 16, RANK)

    def factor_unit(k, slot):
        j, unit = PARTS[k][slot]
        cols = slice(unit * UNIT, (unit + 1) * UNIT)
        product = jnp.dot(left_terms[j][:, 0 : 3 * PADDED[j]], terms[j][:, cols], preferred_element_type=F32)
        partial[k][:, slot * 8 : slot * 8 + 8, :] = product.T.reshape(64, 8, RANK)

    def factor_part(k):
        for slot in range(len(PARTS[k])):
            factor_unit(k, slot)

    def place(ref, base, half, chunk, side):
        return ref.at[pl.ds(base + ((chunk % 4) * 2 + side) * half, half)]

    def setting(k, phase):
        axes = AXES[k % 3]
        first = coord[axes[0]]
        axis = axes[phase - 1]
        return axis, coord[axis], 16 * first

    def reduce_start(k, phase):
        axis, i, base = setting(k, phase)
        base, half, inbox = (0, 8, inbox1[k]) if phase == 1 else (base, 2, inbox2[k])
        at = functools.partial(place, partial[k], base, half)
        n = 0 if phase == 1 else 6
        up, down = device(axis, 1), device(axis, 3)
        return [
            send((k, n), at(i + 2, 0), inbox.at[0], up),
            send((k, n + 1), at(i + 2, 1), inbox.at[1], down),
            send((k, n + 2), at(i + 1, 1), inbox.at[2], up),
            send((k, n + 3), at(i + 3, 0), inbox.at[3], down),
        ]

    def reduce_relay(k, phase, copies):
        axis, i, base = setting(k, phase)
        base, half, inbox = (0, 8, inbox1[k]) if phase == 1 else (base, 2, inbox2[k])
        n = 0 if phase == 1 else 6
        for source, chunk, shift in ((0, i + 1, 1), (1, i + 3, 3)):
            copies[source].wait_recv()
            ref = place(partial[k], base, half, chunk, source)

            def add(s, ref=ref, source=source):
                ref[s] += inbox[source, s]

            each(half, add)
            copies.append(send((k, n + 4 + source), ref, inbox.at[4 + source], device(axis, shift)))

    def reduce_finish(k, phase, copies):
        axis, i, base = setting(k, phase)
        base, half, inbox = (0, 8, inbox1[k]) if phase == 1 else (base, 2, inbox2[k])
        for n in (2, 3, 4, 5):
            copies[n].wait_recv()
        for side, near, relayed in ((0, 3, 4), (1, 2, 5)):
            ref = place(partial[k], base, half, i, side)

            def add(s, ref=ref, near=near, relayed=relayed):
                ref[s] += inbox[near, s] + inbox[relayed, s]

            each(half, add)

    def own(k):
        axes = AXES[k % 3]
        return 4 * coord[axes[1]] + coord[axes[2]]

    def last_reduce_start(k):
        axis, i, base = setting(k, 3)
        base = base + 4 * coord[AXES[k % 3][1]]
        return [
            send((k, 11 + s), partial[k].at[base + (i + s) % 4], inbox3[k].at[s - 1], device(axis, s))
            for s in (1, 2, 3)
        ]

    def last_reduce_finish(k, copies):
        for copy in copies:
            copy.wait_recv()
        mine = partial[k][16 * coord[AXES[k % 3][0]] + own(k)]
        summed[k][own(k)] = (mine + inbox3[k][0]) + (inbox3[k][1] + inbox3[k][2])

    def first_gather_start(k):
        axis, _, _ = setting(k, 3)
        ref = summed[k].at[own(k)]
        return [send((k, 14 + s), ref, ref, device(axis, s)) for s in (1, 2, 3)]

    def gather_start(k, phase):
        axis, i, _ = setting(k, phase)
        ref, half, n = (factor[k], 8, 24) if phase == 1 else (summed[k], 2, 18)
        at = functools.partial(place, ref, 0, half)
        up, down = device(axis, 1), device(axis, 3)
        return [
            send((k, n), at(i, 0), at(i, 0), up),
            send((k, n + 1), at(i, 1), at(i, 1), down),
            send((k, n + 2), at(i, 1), at(i, 1), up),
            send((k, n + 3), at(i, 0), at(i, 0), down),
        ]

    def gather_relay(k, phase, copies):
        axis, i, _ = setting(k, phase)
        ref, half, n = (factor[k], 8, 24) if phase == 1 else (summed[k], 2, 18)
        at = functools.partial(place, ref, 0, half)
        copies[0].wait_recv()
        copies.append(send((k, n + 4), at(i + 3, 0), at(i + 3, 0), device(axis, 1)))
        copies[1].wait_recv()
        copies.append(send((k, n + 5), at(i + 1, 1), at(i + 1, 1), device(axis, 3)))

    def gather_finish(k, copies):
        for n in (2, 3, 4, 5):
            copies[n].wait_recv()

    def apply_inverse(k):
        base = 16 * coord[AXES[k % 3][0]]
        for slot, (j, _) in enumerate(PARTS[k]):
            rows = slice(slot * 8, slot * 8 + 8)
            value = summed[k][:, rows, :].reshape(128, RANK)
            factor[k][pl.ds(base, 16), rows, :] = nt_dot(value, inverse[j], HIGHEST).reshape(16, 8, RANK)

    def gram_scatter():
        x = coord[0]
        return [
            misc(2 + s, gram.at[core, (x + s) % 4], gram_in1.at[x], device(0, s)) for s in (1, 2, 3)
        ]

    def gram_exchange(copies, own_value, box, sent, axis, n):
        for copy in copies:
            copy.wait_recv()
        box_before, at_before = own_value
        box_before[at_before] = sent[0][...]
        sent[1][...] = (box_before[0] + box_before[1]) + (box_before[2] + box_before[3])
        return [misc(n + s, sent[1], box.at[coord[axis]], device(axis, s)) for s in (1, 2, 3)]

    def gram_gather(copies):
        x = coord[0]
        for copy in copies:
            copy.wait_recv()
        gram_in3[coord[2]] = gram_sum[1]
        ref = gram_all.at[core, x]
        ref[...] = (gram_in3[0] + gram_in3[1]) + (gram_in3[2] + gram_in3[3])
        return [misc(11 + s, ref, ref, device(0, s)) for s in (1, 2, 3)]

    def gram_swap(copies):
        for copy in copies:
            copy.wait_recv()
        return misc(15, gram_all.at[core], gram_all.at[core], partner)

    lane = lax.broadcasted_iota(jnp.int32, (8, RANK), 1)
    sublane = lax.broadcasted_iota(jnp.int32, (8, RANK), 0)

    def gram_finish(copy):
        copy.wait_recv()
        row = lax.broadcasted_iota(jnp.int32, (RANK, RANK), 0)
        col = lax.broadcasted_iota(jnp.int32, (RANK, RANK), 1)
        for j in range(3):
            matrix[j, :, 0:RANK] = gram_all[:, :, j].reshape(RANK, RANK)
            matrix[j, :, RANK:] = (row == col).astype(F32)

    def eliminate(block):
        first = pl.multiple_of(block * 8, 8)
        panels = []
        for j in range(3):
            both = matrix[j, pl.ds(first, 8), :]
            panels.append([pltpu.roll(both[:, 0:RANK], (RANK - first) % RANK, 1), both[:, RANK:]])
        for step in range(8):
            for j in range(3):
                a, x = panels[j]
                pivot = jnp.broadcast_to(a[step : step + 1, step : step + 1], (8, RANK))
                scale = 1.0 / jnp.sqrt(pivot)
                column = jnp.broadcast_to(a[:, step : step + 1], (8, RANK)) * scale
                column = jnp.where(sublane > step, column, 0.0)
                row_a = jnp.broadcast_to(a[step : step + 1, :], (8, RANK)) * scale
                row_x = jnp.broadcast_to(x[step : step + 1, :], (8, RANK)) * scale
                here = sublane == step
                panels[j] = [
                    jnp.where(here, row_a, a - column * row_a),
                    jnp.where(here, row_x, x - column * row_x),
                ]
        for j in range(3):
            a, x = panels[j]
            a = pltpu.roll(a, first, 1)
            a = jnp.where(lane >= first + 8, a, 0.0)
            inverse[j, pl.ds(first, 8), :] = x
            matrix[j] = matrix[j] - tn_dot(a, jnp.concatenate([a, x], axis=1), HIGHEST)

    def eliminate_blocks(start, stop):
        def step(block, carry):
            eliminate(block)
            return carry

        lax.fori_loop(start, stop, step, 0)

    wave0 = (0, 1, 2)
    wave1 = (3, 4, 5)
    flying = {}

    pl.semaphore_wait(barrier, len(peers))
    left_copies = [left_partial(0), left_partial(1)]
    left_finish(0, left_copies[0])
    factor_part(0)
    flying[0] = reduce_start(0, 1)
    left_finish(1, left_copies[1])
    for k in (1, 2):
        factor_part(k)
        flying[k] = reduce_start(k, 1)
    left_copies.append(left_partial(2))
    for j in (0, 1):
        gram_partial(j)
    left_finish(2, left_copies[2])
    gram_partial(2)
    gram_copies = gram_scatter()
    for k in wave0:
        reduce_relay(k, 1, flying[k])
    for k in wave1:
        factor_part(k)
        flying[k] = reduce_start(k, 1)
    gram_copies = gram_exchange(gram_copies, (gram_in1, coord[0]), gram_in2, (gram.at[core, coord[0]], gram_sum.at[0]), 1, 5)
    for k in wave0:
        reduce_finish(k, 1, flying[k])
        flying[k] = reduce_start(k, 2)
    gram_copies = gram_exchange(gram_copies, (gram_in2, coord[1]), gram_in3, (gram_sum.at[0], gram_sum.at[1]), 2, 8)
    for k in wave0:
        reduce_relay(k, 2, flying[k])
    for k in wave1:
        reduce_relay(k, 1, flying[k])
    gram_copies = gram_gather(gram_copies)
    for k in wave0:
        reduce_finish(k, 2, flying[k])
        flying[k] = last_reduce_start(k)
    gram_copy = gram_swap(gram_copies)
    gram_finish(gram_copy)
    eliminate_blocks(0, 4)
    for k in wave0:
        last_reduce_finish(k, flying[k])
        flying[k] = first_gather_start(k)
    for k in wave1:
        reduce_finish(k, 1, flying[k])
        flying[k] = reduce_start(k, 2)
    eliminate_blocks(4, 7)
    for k in wave0:
        gather_finish_direct(flying[k])
        flying[k] = gather_start(k, 2)
    for k in wave1:
        reduce_relay(k, 2, flying[k])
    eliminate_blocks(7, 10)
    for k in wave0:
        gather_relay(k, 2, flying[k])
    for k in wave1:
        reduce_finish(k, 2, flying[k])
        flying[k] = last_reduce_start(k)
    eliminate_blocks(10, 16)
    for k in wave0:
        gather_finish(k, flying[k])
        apply_inverse(k)
        flying[k] = gather_start(k, 1)
    for k in wave1:
        last_reduce_finish(k, flying[k])
        flying[k] = first_gather_start(k)
    for j in range(3):
        basis[j][...] = nt_dot(left_in[j][...], inverse[j], HIGHEST)[0 : ROWS[j]]
    for k in wave1:
        gather_finish_direct(flying[k])
        flying[k] = gather_start(k, 2)
    for k in wave0:
        gather_relay(k, 1, flying[k])
    for k in wave1:
        gather_relay(k, 2, flying[k])
    for k in wave1:
        gather_finish(k, flying[k])
        apply_inverse(k)
        flying[k] = gather_start(k, 1)
    for k in wave0:
        gather_finish(k, flying[k])
    sums = [jnp.zeros((8, RANK), F32) for _ in range(3)]

    def add_squares(k, sums):
        for slot, (j, _) in enumerate(PARTS[k]):
            def step(i, total, slot=slot):
                value = factor[k][pl.ds(i * 8, 8), slot * 8 : slot * 8 + 8, :]
                return total + jnp.sum(value * value, axis=0)

            sums[j] = lax.fori_loop(0, 8, step, sums[j])

    for k in wave0:
        add_squares(k, sums)
    for k in wave1:
        gather_relay(k, 1, flying[k])
    for k in wave1:
        gather_finish(k, flying[k])
        add_squares(k, sums)
    rows = [jnp.sum(value, axis=0, keepdims=True) for value in sums]
    squares_in[0] = jnp.concatenate(rows + [jnp.zeros((5, RANK), F32)], axis=0)
    copy = misc(16, squares_in.at[0], squares_in.at[1], partner)
    copy.wait_recv()
    squares[...] = squares_in[0] + squares_in[1]
    for copy in started:
        copy.wait_send()


def gather_finish_direct(copies):
    for copy in copies:
        copy.wait_recv()


def update_kernel(
    weight,
    factor,
    buffer,
    basis,
    squares,
    moment_out,
    weight_out,
    right_out,
    change_out,
    weight_in,
    moment_box,
    weight_box,
    right_box,
    change_box,
    rows_in,
    load_sem,
    store_sem,
):
    loads = [pltpu.make_async_copy(weight[j], weight_in[j], load_sem.at[j]) for j in range(3)]
    for copy in loads:
        copy.start()
    scale = 1.0 / (jnp.sqrt(squares[...]) + EPSILON)
    for j in range(3):
        rows, pad = ROWS[j], PADDED[j]
        value = basis[j][...]
        if pad > rows:
            value = jnp.concatenate([value, jnp.zeros((pad - rows, RANK), F32)], axis=0)
        step_size = LEARN_RATE * math.sqrt(SHAPE[j][0] / SHAPE[j][1])
        high, low = split(value * (scale[j : j + 1] * step_size))
        rows_in[j][0:pad, 0:RANK] = high
        rows_in[j][0:pad, RANK:] = high
        rows_in[j][pad : 2 * pad, 0:RANK] = low
        rows_in[j][pad : 2 * pad, RANK:] = jnp.zeros((pad, RANK), BF16)
        moment = (value * (1.0 - DECAY)).astype(BF16)
        rows_in[j][2 * pad :, 0:RANK] = moment
        rows_in[j][2 * pad :, RANK:] = jnp.zeros((pad, RANK), BF16)
    waited = [False] * 3
    stores = []
    for k in range(N_PARTS):
        for slot, (j, unit) in enumerate(PARTS[k]):
            if not waited[j]:
                loads[j].wait()
                waited[j] = True
            rows, pad = ROWS[j], PADDED[j]
            start = unit * UNIT
            width = min(UNIT, COLS[j] - start)
            value = factor[k][0 : width // 8, slot * 8 : slot * 8 + 8, :].reshape(width, RANK)
            cols = slice(start, start + width)
            right_box[j][cols, :] = value * scale[j : j + 1]
            high, low = split(value)
            product = nt_dot(rows_in[j][...], jnp.concatenate([high, low], axis=1))
            change = product[0:rows] + product[pad : pad + rows]
            change_box[j][:, cols] = change
            moment_box[j][:, cols] = buffer[j][:, cols] - product[2 * pad : 2 * pad + rows]
            weight_box[j][:, cols] = (weight_in[j][:, cols].astype(F32) - change).astype(BF16)
            pairs = (
                (right_box[j].at[cols, :], right_out[j].at[cols, :]),
                (change_box[j].at[:, cols], change_out[j].at[:, cols]),
                (moment_box[j].at[:, cols], moment_out[j].at[:, cols]),
                (weight_box[j].at[:, cols], weight_out[j].at[:, cols]),
            )
            for n, (src, dst) in enumerate(pairs):
                copy = pltpu.make_async_copy(src, dst, store_sem.at[k, slot, n])
                copy.start()
                stores.append(copy)
    for copy in stores:
        copy.wait()


def local(
    out_momentum,
    out_gradient,
    out_weight,
    out_right,
    up_momentum,
    up_gradient,
    up_weight,
    up_right,
    down_momentum,
    down_gradient,
    down_weight,
    down_right,
):
    momentum = [down_momentum, out_momentum, up_momentum]
    gradient = [down_gradient, out_gradient, up_gradient]
    weight = [down_weight, out_weight, up_weight]
    right = [down_right, out_right, up_right]
    vmem = pltpu.VMEM
    anywhere = pl.BlockSpec(memory_space=pl.ANY)
    inside = pl.BlockSpec(memory_space=vmem)
    dma = pltpu.SemaphoreType.DMA
    each_part = lambda lead: [vmem((*lead, HEIGHT[k], RANK), F32) for k in range(N_PARTS)]

    factor_shapes = [jax.ShapeDtypeStruct((64, HEIGHT[k], RANK), F32) for k in range(N_PARTS)]
    buffer_shapes = [jax.ShapeDtypeStruct((ROWS[j], COLS[j]), F32) for j in range(3)]
    basis_shapes = [jax.ShapeDtypeStruct((ROWS[j], RANK), F32) for j in range(3)]
    middle = [factor_shapes, buffer_shapes, basis_shapes, jax.ShapeDtypeStruct((8, RANK), F32)]
    placed = jax.tree.map(lambda s: vmem(s.shape, s.dtype), middle)
    terms_cols = [UNIT * count for count in UNITS]
    factor, buffer, basis, squares = pl.pallas_call(
        reduce_kernel,
        out_shape=placed,
        in_specs=[[anywhere] * 3] * 3,
        out_specs=jax.tree.map(lambda s: inside, middle),
        scratch_shapes=[
            each_part((64,)),
            each_part((16,)),
            each_part((6, 8)),
            each_part((6, 2)),
            each_part((3,)),
            [vmem((ROWS[j], COLS[j]), BF16) for j in range(3)],
            [vmem((COLS[j], RANK), F32) for j in range(3)],
            [vmem((3 * PADDED[j], terms_cols[j]), BF16) for j in range(3)],
            [vmem((COLS[j], 2 * RANK), BF16) for j in range(3)],
            [vmem((PADDED[j], RANK), F32) for j in range(3)],
            [vmem((PADDED[j], RANK), F32) for j in range(3)],
            [vmem((RANK, TERMS[j]), BF16) for j in range(3)],
            vmem((2, 4, 3, 16, RANK), F32),
            vmem((4, 3, 16, RANK), F32),
            vmem((4, 3, 16, RANK), F32),
            vmem((4, 3, 16, RANK), F32),
            vmem((2, 3, 16, RANK), F32),
            vmem((2, 4, 3, 16, RANK), F32),
            vmem((3, RANK, 2 * RANK), F32),
            vmem((3, RANK, RANK), F32),
            vmem((2, 8, RANK), F32),
            dma((3, 3, 3)),
            dma((N_PARTS, 30)),
            dma((N_PARTS, 30)),
            dma((17,)),
            dma((17,)),
        ],
        compiler_params=pltpu.CompilerParams(
            collective_id=0, has_side_effects=True, vmem_limit_bytes=50 * 2**20
        ),
        name="reduce",
    )(momentum, gradient, right)
    keep = lambda x: pltpu.with_memory_space_constraint(x, vmem)
    factor, buffer, basis, squares = jax.tree.map(keep, (factor, buffer, basis, squares))
    matrices = lambda dtype: [jax.ShapeDtypeStruct((ROWS[j], COLS[j]), dtype) for j in range(3)]
    factors = [jax.ShapeDtypeStruct((COLS[j], RANK), F32) for j in range(3)]
    results = [matrices(F32), matrices(BF16), factors, matrices(F32)]
    moment, weight, right, change = pl.pallas_call(
        update_kernel,
        out_shape=results,
        in_specs=[[anywhere] * 3, [inside] * N_PARTS, [inside] * 3, [inside] * 3, inside],
        out_specs=jax.tree.map(lambda s: anywhere, results),
        scratch_shapes=[
            [vmem((ROWS[j], COLS[j]), BF16) for j in range(3)],
            [vmem((ROWS[j], COLS[j]), F32) for j in range(3)],
            [vmem((ROWS[j], COLS[j]), BF16) for j in range(3)],
            [vmem((COLS[j], RANK), F32) for j in range(3)],
            [vmem((ROWS[j], COLS[j]), F32) for j in range(3)],
            [vmem((3 * PADDED[j], 2 * RANK), BF16) for j in range(3)],
            dma((3,)),
            dma((N_PARTS, max(PER_PART), 4)),
        ],
        compiler_params=pltpu.CompilerParams(vmem_limit_bytes=44 * 2**20),
        name="update",
    )(weight, factor, buffer, basis, squares)
    pick = lambda group: (group[1], group[2], group[0])
    return (*pick(moment), *pick(weight), *pick(right), *pick(change))


def solution(mesh):
    matrix, factor = P(("fsdp", "rep"), "tp"), P("tp", None)
    in_specs = (matrix, matrix, matrix, factor) * 3
    out_specs = (matrix,) * 6 + (factor,) * 3 + (matrix,) * 3
    return jax.shard_map(local, mesh=mesh, in_specs=in_specs, out_specs=out_specs, check_vma=False)
```

```python
import functools
import math

import jax
import jax.numpy as jnp
from jax import lax
from jax.experimental import pallas as pl
from jax.experimental.pallas import tpu as pltpu
from jax.sharding import PartitionSpec as P

ROWS = (216, 80, 80)
PADDED = (224, 80, 80)
COLS = (2560, 2560, 6912)
UNITS = (5, 5, 14)
SPANS = ((1280, 1280), (1280, 1280), (2304, 2304, 2304))
SHAPE = ((13824, 5120), (5120, 5120), (5120, 13824))
UNIT = 512
RANK = 128
DECAY = 0.95
LEARN_RATE = 0.02
EPSILON = 1e-08
MESH = pl.DeviceIdType.MESH
F32 = jnp.float32
BF16 = jnp.bfloat16
HIGHEST = lax.Precision.HIGHEST
AXES = ((0, 1, 2), (1, 2, 0), (2, 0, 1))
TERMS = tuple(3 * rows + (-3 * rows) % 128 for rows in PADDED)

PER_PART = (3, 5)


def make_parts():
    units = [(matrix, unit) for matrix in range(3) for unit in range(UNITS[matrix])]
    parts = []
    for count in PER_PART:
        for _ in range(3):
            parts.append(units[:count])
            units = units[count:]
    return parts


PARTS = make_parts()
N_PARTS = len(PARTS)
GROUPS = ((1, (0, 1)), (1, (2, 3)), (1, (4,)), (0, (0, 1)), (0, (2, 3)), (0, (4,))) + tuple(
    (2, (unit, unit + 1)) for unit in range(0, 14, 2)
)
PLAN = (
    ("left", 0),
    ("left", 1),
    ("finish", 0),
    ("finish", 1),
    ("R1a", 0),
    ("left", 2),
    ("finish", 2),
    ("gram", 0),
    ("R1b", 0),
    ("gram", 1),
    ("R1a", 1),
    ("gram", 2),
    ("R1c", 0),
    ("gram", 3),
    ("R2b", 0),
    ("gram", 4),
    ("R1b", 1),
    ("gram", 5),
    ("chol", 0),
    ("R2c", 0),
    ("chol", 1),
    ("R1c", 1),
    ("R3c", 0),
    ("chol", 2),
    ("R2b", 1),
    ("chol", 3),
    ("G3c", 0),
    ("chol", 4),
    ("R2c", 1),
    ("G2b", 0),
    ("chol", 5),
    ("R3c", 1),
    ("chol", 6),
    ("chol", 7),
    ("G2c", 0),
    ("G3c", 1),
    ("G1b", 0),
    ("G2b", 1),
    ("G2c", 1),
    ("G1c", 0),
    ("G1b", 1),
    ("G1c", 1),
)
HEIGHT = [8 * len(part) for part in PARTS]


def split(value):
    high = value.astype(BF16)
    return high, (value - high.astype(F32)).astype(BF16)


def nt_dot(first, second, precision=None):
    return lax.dot_general(first, second, (((1,), (1,)), ((), ())), precision=precision, preferred_element_type=F32)


def tn_dot(first, second, precision=None):
    return lax.dot_general(first, second, (((0,), (0,)), ((), ())), precision=precision, preferred_element_type=F32)


def each(count, body):
    def step(index, carry):
        body(index)
        return carry

    lax.fori_loop(0, count, step, 0)


def reduce_kernel(
    momentum,
    gradient,
    right,
    factor,
    buffer,
    basis,
    squares,
    partial,
    summed,
    inbox1,
    inbox2,
    inbox3,
    grad_in,
    right_in,
    terms,
    right_terms,
    left,
    left_in,
    left_terms,
    gram,
    gram_in1,
    gram_in2,
    gram_in3,
    gram_sum,
    gram_all,
    matrix,
    inverse,
    inverse_terms,
    squares_in,
    load_sem,
    send_sem,
    recv_sem,
    misc_send,
    misc_recv,
):
    rows_at = lax.axis_index("fsdp")
    core = lax.axis_index("tp")
    coord = (lax.axis_index("rep"), rows_at % 4, rows_at // 4)

    def device(axis, shift):
        moved = [(coord[a] + shift) % 4 if a == axis else coord[a] for a in range(3)]
        return (moved[2] * 4 + moved[1], core, moved[0])

    partner = (rows_at, 1 - core, coord[0])

    loads = []
    for j in range(3):
        steps = []
        start = 0
        for s, span in enumerate(SPANS[j]):
            cols = pl.ds(start, span)
            copies = [
                pltpu.make_async_copy(momentum[j].at[:, cols], buffer[j].at[:, cols], load_sem.at[j, s, 0]),
                pltpu.make_async_copy(gradient[j].at[:, cols], grad_in[j].at[:, cols], load_sem.at[j, s, 1]),
                pltpu.make_async_copy(right[j].at[cols, :], right_in[j].at[cols, :], load_sem.at[j, s, 2]),
            ]
            for copy in copies:
                copy.start()
            steps.append((start, span, copies))
            start += span
        loads.append(steps)

    barrier = pltpu.get_barrier_semaphore()
    peers = [device(axis, shift) for axis in range(3) for shift in (1, 2, 3)] + [partner]
    for peer in peers:
        pl.semaphore_signal(barrier, inc=1, device_id=peer, device_id_type=MESH)

    started = []

    def send(first, second, src, dst, target):
        copy = pltpu.make_async_remote_copy(
            src_ref=src, dst_ref=dst, send_sem=first, recv_sem=second, device_id=target, device_id_type=MESH
        )
        copy.start()
        return copy

    def misc(index, src, dst, target):
        copy = send(misc_send.at[index], misc_recv.at[index], src, dst, target)
        started.append(copy)
        return copy

    def wait_all(ref, sem):
        pltpu.make_async_copy(ref, ref, sem).wait()

    def left_partial(j):
        pad = PADDED[j]
        total = None
        for start, span, copies in loads[j]:
            for copy in copies:
                copy.wait()

            def prepare(i, start=start):
                cols = pl.ds(pl.multiple_of(start + i * 256, 256), 256)
                value = buffer[j][:, cols] + grad_in[j][:, cols].astype(F32)
                buffer[j][:, cols] = value
                if pad > ROWS[j]:
                    value = jnp.concatenate([value, jnp.zeros((pad - ROWS[j], 256), F32)], axis=0)
                high, low = split(value)
                terms[j][0:pad, cols] = high
                terms[j][pad : 2 * pad, cols] = low
                terms[j][2 * pad : 3 * pad, cols] = high
                high, low = split(right_in[j][cols, :])
                right_terms[j][cols, 0:RANK] = high
                right_terms[j][cols, RANK : 2 * RANK] = low

            each(span // 256, prepare)
            product = jnp.dot(
                terms[j][0 : 2 * pad, start : start + span],
                right_terms[j][start : start + span, :],
                preferred_element_type=F32,
            )
            product = product[0:pad, 0:RANK] + (product[0:pad, RANK:] + product[pad:, 0:RANK])
            total = product if total is None else total + product
        left[j][...] = total
        if terms[j].shape[1] > COLS[j]:
            terms[j][:, COLS[j] :] = jnp.zeros((3 * pad, terms[j].shape[1] - COLS[j]), BF16)
        return misc(j, left[j], left_in[j], partner)

    def left_finish(j, copy):
        copy.wait_recv()
        pad = PADDED[j]
        value = left[j][...] + left_in[j][...]
        left_in[j][...] = value
        high = value.astype(BF16).astype(F32)
        low = value - high
        pieces = [high, high, low]
        if TERMS[j] > 3 * pad:
            pieces.append(jnp.zeros((TERMS[j] - 3 * pad, RANK), F32))
        left_terms[j][...] = jnp.concatenate(pieces, axis=0).T.astype(BF16)

    def gram_partial(j):
        value = left_in[j][...]
        result = tn_dot(value, value, HIGHEST)
        gram[:, :, j] = result.reshape(2, 4, 16, RANK)

    def factor_unit(k, slot):
        j, unit = PARTS[k][slot]
        cols = slice(unit * UNIT, (unit + 1) * UNIT)
        product = jnp.dot(left_terms[j][:, 0 : 3 * PADDED[j]], terms[j][:, cols], preferred_element_type=F32)
        partial[k][:, slot * 8 : slot * 8 + 8, :] = product.T.reshape(64, 8, RANK)

    def factor_part(k):
        for slot in range(len(PARTS[k])):
            factor_unit(k, slot)

    def place(ref, base, half, chunk, side):
        return ref.at[pl.ds(base + ((chunk % 4) * 2 + side) * half, half)]

    def first_coord(k):
        return coord[AXES[k % 3][0]]

    def reduce_setting(k, phase):
        axis = AXES[k % 3][phase - 1]
        base, half, inbox = (0, 8, inbox1[k]) if phase == 1 else (16 * first_coord(k), 2, inbox2[k])
        at = functools.partial(place, partial[k], base, half)

        def out(n, ref, box, shift):
            sem = recv_sem.at[k, 3 * (phase - 1) + min(n, 2)]
            send(send_sem.at[k, 0], sem, ref, inbox.at[box], device(axis, shift))

        return coord[axis], at, half, inbox, out

    def reduce_start(k, phase):
        i, at, half, inbox, out = reduce_setting(k, phase)
        out(0, at(i + 2, 0), 0, 1)
        out(1, at(i + 2, 1), 1, 3)
        out(2, at(i + 1, 1), 2, 1)
        out(2, at(i + 3, 0), 3, 3)

    def reduce_relay(k, phase):
        i, at, half, inbox, out = reduce_setting(k, phase)
        for side, chunk, shift in ((0, i + 1, 1), (1, i + 3, 3)):
            wait_all(inbox.at[side], recv_sem.at[k, 3 * (phase - 1) + side])
            ref = at(chunk, side)

            def add(s, ref=ref, side=side):
                ref[s] += inbox[side, s]

            each(half, add)
            out(2, ref, 4 + side, shift)

    def reduce_finish(k, phase):
        i, at, half, inbox, out = reduce_setting(k, phase)
        wait_all(inbox.at[2:6], recv_sem.at[k, 3 * (phase - 1) + 2])
        for side, near, relayed in ((0, 3, 4), (1, 2, 5)):
            ref = at(i, side)

            def add(s, ref=ref, near=near, relayed=relayed):
                ref[s] += inbox[near, s] + inbox[relayed, s]

            each(half, add)

    def own(k):
        axes = AXES[k % 3]
        return 4 * coord[axes[1]] + coord[axes[2]]

    def last_reduce_start(k):
        axes = AXES[k % 3]
        base, i = 16 * coord[axes[0]] + 4 * coord[axes[1]], coord[axes[2]]
        for s in (1, 2, 3):
            ref = partial[k].at[base + (i + s) % 4]
            send(send_sem.at[k, 0], recv_sem.at[k, 6], ref, inbox3[k].at[s - 1], device(axes[2], s))

    def last_reduce_finish(k):
        wait_all(inbox3[k], recv_sem.at[k, 6])
        mine = partial[k][16 * first_coord(k) + own(k)]
        summed[k][own(k)] = (mine + inbox3[k][0]) + (inbox3[k][1] + inbox3[k][2])

    def first_gather_start(k):
        ref = summed[k].at[own(k)]
        for s in (1, 2, 3):
            send(send_sem.at[k, 1], recv_sem.at[k, 7], ref, ref, device(AXES[k % 3][2], s))

    def first_gather_finish(k):
        wait_all(summed[k].at[0:3], recv_sem.at[k, 7])

    def gather_setting(k, phase):
        axis = AXES[k % 3][phase - 1]
        ref, half, first = (factor[k], 8, 11) if phase == 1 else (summed[k], 2, 8)
        at = functools.partial(place, ref, 0, half)

        def out(n, there, shift):
            send(send_sem.at[k, 1], recv_sem.at[k, first + n], there, there, device(axis, shift))

        def arrived(n):
            wait_all(ref.at[0:half] if n < 2 else ref.at[0 : 4 * half], recv_sem.at[k, first + n])

        return coord[axis], at, out, arrived

    def gather_start(k, phase):
        i, at, out, arrived = gather_setting(k, phase)
        out(0, at(i, 0), 1)
        out(1, at(i, 1), 3)
        out(2, at(i, 1), 1)
        out(2, at(i, 0), 3)

    def gather_relay(k, phase):
        i, at, out, arrived = gather_setting(k, phase)
        arrived(0)
        out(2, at(i + 3, 0), 1)
        arrived(1)
        out(2, at(i + 1, 1), 3)

    def gather_finish(k, phase):
        gather_setting(k, phase)[3](2)

    def apply_inverse(k):
        base = 16 * first_coord(k)
        for j in range(3):
            slots = [slot for slot, (other, _) in enumerate(PARTS[k]) if other == j]
            if not slots:
                continue
            rows = slice(slots[0] * 8, slots[-1] * 8 + 8)
            count = 8 * len(slots)
            high, low = split(summed[k][:, rows, :].reshape(16 * count, RANK))
            product = nt_dot(jnp.concatenate([high, low], axis=0), inverse_terms[j])
            product = product[: 16 * count, :RANK] + (product[: 16 * count, RANK:] + product[16 * count :, :RANK])
            factor[k][pl.ds(base, 16), rows, :] = product.reshape(16, count, RANK)

    def gram_scatter():
        x = coord[0]
        return [
            misc(2 + s, gram.at[core, (x + s) % 4], gram_in1.at[x], device(0, s)) for s in (1, 2, 3)
        ]

    def gram_exchange(copies, own_value, box, sent, axis, n):
        for copy in copies:
            copy.wait_recv()
        box_before, at_before = own_value
        box_before[at_before] = sent[0][...]
        sent[1][...] = (box_before[0] + box_before[1]) + (box_before[2] + box_before[3])
        return [misc(n + s, sent[1], box.at[coord[axis]], device(axis, s)) for s in (1, 2, 3)]

    def gram_gather(copies):
        x = coord[0]
        for copy in copies:
            copy.wait_recv()
        gram_in3[coord[2]] = gram_sum[1]
        ref = gram_all.at[core, x]
        ref[...] = (gram_in3[0] + gram_in3[1]) + (gram_in3[2] + gram_in3[3])
        return [misc(11 + s, ref, ref, device(0, s)) for s in (1, 2, 3)]

    def gram_swap(copies):
        for copy in copies:
            copy.wait_recv()
        return misc(15, gram_all.at[core], gram_all.at[core], partner)

    def gram_finish(copy):
        copy.wait_recv()
        row = lax.broadcasted_iota(jnp.int32, (RANK, RANK), 0)
        col = lax.broadcasted_iota(jnp.int32, (RANK, RANK), 1)
        for j in range(3):
            matrix[j, :, 0:RANK] = gram_all[:, :, j].reshape(RANK, RANK)
            matrix[j, :, RANK:] = (row == col).astype(F32)

    def eliminate(piece):
        first, start = piece // 4 * 32, piece * 8
        stop = first + 32
        count = stop - start
        a = matrix[:, start:stop, 0:RANK]
        x = matrix[:, start:stop, RANK:]
        rows = lax.broadcasted_iota(jnp.int32, (3, count, RANK), 1)
        columns = [jnp.broadcast_to(a[:, :, start + n : start + n + 1], (3, count, RANK)) for n in range(8)]
        pivots = []
        for n in range(8):
            pivot = columns[n][:, n : n + 1, :]
            pivots.append(pivot)
            scale = 1.0 / jnp.broadcast_to(pivot, (3, 8, RANK))
            ratio = jnp.where(rows > n, columns[n] * scale[:, 0:1, :], 0.0)
            for later in range(n + 1, 8):
                columns[later] = columns[later] - ratio * columns[later][:, n : n + 1, :]
            a = a - ratio * a[:, n : n + 1, :]
            x = x - ratio * x[:, n : n + 1, :]
        scale = 1.0 / jnp.sqrt(jnp.concatenate(pivots, axis=1))
        matrix[:, start : start + 8, 0:RANK] = a[:, 0:8] * scale
        inverse[:, start : start + 8, :] = x[:, 0:8] * scale
        if count > 8:
            matrix[:, start + 8 : stop, 0:RANK] = a[:, 8:]
            matrix[:, start + 8 : stop, RANK:] = x[:, 8:]
        elif stop < RANK:
            lane = lax.broadcasted_iota(jnp.int32, (32, RANK), 1)
            for j in range(3):
                panel = jnp.where(lane >= stop, matrix[j, first:stop, 0:RANK], 0.0)
                both = jnp.concatenate([panel, inverse[j, first:stop, :]], axis=1)
                matrix[j, stop:] = matrix[j, stop:] - tn_dot(panel, both, HIGHEST)[stop:]
        else:
            for j in range(3):
                high, low = split(inverse[j])
                inverse_terms[j, 0:RANK] = high
                inverse_terms[j, RANK:] = low

    def basis_all():
        for j in range(3):
            basis[j][...] = nt_dot(left_in[j][...], inverse[j], HIGHEST)[0 : ROWS[j]]

    sums = [jnp.zeros((8, RANK), F32) for _ in range(3)]

    def add_squares(k):
        for slot, (j, _) in enumerate(PARTS[k]):

            def step(i, total, slot=slot):
                value = factor[k][pl.ds(i * 8, 8), slot * 8 : slot * 8 + 8, :]
                return total + jnp.sum(value * value, axis=0)

            sums[j] = lax.fori_loop(0, 8, step, sums[j])

    held = {}

    def run(name, value):
        parts = range(3 * value, 3 * value + 3)
        if name == "left":
            held["left", value] = left_partial(value)
        elif name == "finish":
            left_finish(value, held["left", value])
        elif name == "gram":
            if value == 0:
                for j in range(3):
                    gram_partial(j)
                held["gram"] = gram_scatter()
            elif value == 1:
                sent = (gram.at[core, coord[0]], gram_sum.at[0])
                held["gram"] = gram_exchange(held["gram"], (gram_in1, coord[0]), gram_in2, sent, 1, 5)
            elif value == 2:
                sent = (gram_sum.at[0], gram_sum.at[1])
                held["gram"] = gram_exchange(held["gram"], (gram_in2, coord[1]), gram_in3, sent, 2, 8)
            elif value == 3:
                held["gram"] = gram_gather(held["gram"])
            elif value == 4:
                held["gram"] = gram_swap(held["gram"])
            else:
                gram_finish(held["gram"])
        elif name == "chol":
            for piece in range(2 * value, 2 * value + 2):
                eliminate(piece)
            if value == 7:
                basis_all()
        for k in parts:
            if name == "R1a":
                factor_part(k)
                reduce_start(k, 1)
            elif name == "R1b":
                reduce_relay(k, 1)
            elif name == "R1c":
                reduce_finish(k, 1)
                reduce_start(k, 2)
            elif name == "R2b":
                reduce_relay(k, 2)
            elif name == "R2c":
                reduce_finish(k, 2)
                last_reduce_start(k)
            elif name == "R3c":
                last_reduce_finish(k)
                first_gather_start(k)
            elif name == "G3c":
                first_gather_finish(k)
                gather_start(k, 2)
            elif name == "G2b":
                gather_relay(k, 2)
            elif name == "G2c":
                gather_finish(k, 2)
                apply_inverse(k)
                gather_start(k, 1)
            elif name == "G1b":
                gather_relay(k, 1)
            elif name == "G1c":
                gather_finish(k, 1)
                add_squares(k)

    pl.semaphore_wait(barrier, len(peers))
    for name, value in PLAN:
        run(name, value)
    rows = [jnp.sum(value, axis=0, keepdims=True) for value in sums]
    squares_in[0] = jnp.concatenate(rows + [jnp.zeros((5, RANK), F32)], axis=0)
    copy = misc(16, squares_in.at[0], squares_in.at[1], partner)
    for k in range(N_PARTS):
        for side in range(2):
            wait_all(partial[k].at[0:63], send_sem.at[k, side])
    copy.wait_recv()
    squares[...] = squares_in[0] + squares_in[1]
    for copy in started:
        copy.wait_send()


def update_kernel(
    weight,
    factor,
    buffer,
    basis,
    squares,
    moment_out,
    weight_out,
    right_out,
    change_out,
    weight_in,
    moment_box,
    weight_box,
    right_box,
    change_box,
    rows_in,
    load_sem,
    store_sem,
):
    loads = [pltpu.make_async_copy(weight[j], weight_in[j], load_sem.at[j]) for j in range(3)]
    for copy in loads:
        copy.start()
    scale = 1.0 / (jnp.sqrt(squares[...]) + EPSILON)
    for j in range(3):
        rows, pad = ROWS[j], PADDED[j]
        value = basis[j][...]
        if pad > rows:
            value = jnp.concatenate([value, jnp.zeros((pad - rows, RANK), F32)], axis=0)
        step_size = LEARN_RATE * math.sqrt(SHAPE[j][0] / SHAPE[j][1])
        high, low = split(value * (scale[j : j + 1] * step_size))
        rows_in[j][0:pad, 0:RANK] = high
        rows_in[j][0:pad, RANK:] = high
        rows_in[j][pad : 2 * pad, 0:RANK] = low
        rows_in[j][pad : 2 * pad, RANK:] = jnp.zeros((pad, RANK), BF16)
        moment = (value * (1.0 - DECAY)).astype(BF16)
        rows_in[j][2 * pad :, 0:RANK] = moment
        rows_in[j][2 * pad :, RANK:] = jnp.zeros((pad, RANK), BF16)
    where = {unit: (k, slot) for k, part in enumerate(PARTS) for slot, unit in enumerate(part)}
    for group, (j, units) in enumerate(GROUPS):
        if units[0] == 0:
            loads[j].wait()
        rows, pad = ROWS[j], PADDED[j]
        for unit in units:
            k, slot = where[j, unit]
            start = unit * UNIT
            width = min(UNIT, COLS[j] - start)
            value = factor[k][0 : width // 8, slot * 8 : slot * 8 + 8, :].reshape(width, RANK)
            cols = slice(start, start + width)
            right_box[j][cols, :] = value * scale[j : j + 1]
            high, low = split(value)
            product = nt_dot(rows_in[j][...], jnp.concatenate([high, low], axis=1))
            change = product[0:rows] + product[pad : pad + rows]
            change_box[j][:, cols] = change
            moment_box[j][:, cols] = buffer[j][:, cols] - product[2 * pad : 2 * pad + rows]
            weight_box[j][:, cols] = (weight_in[j][:, cols].astype(F32) - change).astype(BF16)
        cols = slice(units[0] * UNIT, min(units[-1] * UNIT + UNIT, COLS[j]))
        pltpu.make_async_copy(right_box[j].at[cols, :], right_out[j].at[cols, :], store_sem.at[j, 0]).start()
        for n, (box, out) in enumerate(((change_box, change_out), (moment_box, moment_out), (weight_box, weight_out))):
            pltpu.make_async_copy(box[j].at[:, cols], out[j].at[:, cols], store_sem.at[j, n + 1]).start()
    for j in range(3):
        for n, (box, out) in enumerate(
            ((right_box, right_out), (change_box, change_out), (moment_box, moment_out), (weight_box, weight_out))
        ):
            pltpu.make_async_copy(box[j], out[j], store_sem.at[j, n]).wait()


def local(
    out_momentum,
    out_gradient,
    out_weight,
    out_right,
    up_momentum,
    up_gradient,
    up_weight,
    up_right,
    down_momentum,
    down_gradient,
    down_weight,
    down_right,
):
    momentum = [down_momentum, out_momentum, up_momentum]
    gradient = [down_gradient, out_gradient, up_gradient]
    weight = [down_weight, out_weight, up_weight]
    right = [down_right, out_right, up_right]
    vmem = pltpu.VMEM
    anywhere = pl.BlockSpec(memory_space=pl.ANY)
    inside = pl.BlockSpec(memory_space=vmem)
    dma = pltpu.SemaphoreType.DMA
    each_part = lambda lead: [vmem((*lead, HEIGHT[k], RANK), F32) for k in range(N_PARTS)]

    factor_shapes = [jax.ShapeDtypeStruct((64, HEIGHT[k], RANK), F32) for k in range(N_PARTS)]
    buffer_shapes = [jax.ShapeDtypeStruct((ROWS[j], COLS[j]), F32) for j in range(3)]
    basis_shapes = [jax.ShapeDtypeStruct((ROWS[j], RANK), F32) for j in range(3)]
    middle = [factor_shapes, buffer_shapes, basis_shapes, jax.ShapeDtypeStruct((8, RANK), F32)]
    placed = jax.tree.map(lambda s: vmem(s.shape, s.dtype), middle)
    terms_cols = [UNIT * count for count in UNITS]
    factor, buffer, basis, squares = pl.pallas_call(
        reduce_kernel,
        out_shape=placed,
        in_specs=[[anywhere] * 3] * 3,
        out_specs=jax.tree.map(lambda s: inside, middle),
        scratch_shapes=[
            each_part((64,)),
            each_part((16,)),
            each_part((6, 8)),
            each_part((6, 2)),
            each_part((3,)),
            [vmem((ROWS[j], COLS[j]), BF16) for j in range(3)],
            [vmem((COLS[j], RANK), F32) for j in range(3)],
            [vmem((3 * PADDED[j], terms_cols[j]), BF16) for j in range(3)],
            [vmem((COLS[j], 2 * RANK), BF16) for j in range(3)],
            [vmem((PADDED[j], RANK), F32) for j in range(3)],
            [vmem((PADDED[j], RANK), F32) for j in range(3)],
            [vmem((RANK, TERMS[j]), BF16) for j in range(3)],
            vmem((2, 4, 3, 16, RANK), F32),
            vmem((4, 3, 16, RANK), F32),
            vmem((4, 3, 16, RANK), F32),
            vmem((4, 3, 16, RANK), F32),
            vmem((2, 3, 16, RANK), F32),
            vmem((2, 4, 3, 16, RANK), F32),
            vmem((3, RANK, 2 * RANK), F32),
            vmem((3, RANK, RANK), F32),
            vmem((3, 2 * RANK, RANK), BF16),
            vmem((2, 8, RANK), F32),
            dma((3, 3, 3)),
            dma((N_PARTS, 2)),
            dma((N_PARTS, 14)),
            dma((17,)),
            dma((17,)),
        ],
        compiler_params=pltpu.CompilerParams(
            collective_id=0, has_side_effects=True, vmem_limit_bytes=50 * 2**20
        ),
        name="reduce",
    )(momentum, gradient, right)
    keep = lambda x: pltpu.with_memory_space_constraint(x, vmem)
    factor, buffer, basis, squares = jax.tree.map(keep, (factor, buffer, basis, squares))
    matrices = lambda dtype: [jax.ShapeDtypeStruct((ROWS[j], COLS[j]), dtype) for j in range(3)]
    factors = [jax.ShapeDtypeStruct((COLS[j], RANK), F32) for j in range(3)]
    results = [matrices(F32), matrices(BF16), factors, matrices(F32)]
    moment, weight, right, change = pl.pallas_call(
        update_kernel,
        out_shape=results,
        in_specs=[[anywhere] * 3, [inside] * N_PARTS, [inside] * 3, [inside] * 3, inside],
        out_specs=jax.tree.map(lambda s: anywhere, results),
        scratch_shapes=[
            [vmem((ROWS[j], COLS[j]), BF16) for j in range(3)],
            [vmem((ROWS[j], COLS[j]), F32) for j in range(3)],
            [vmem((ROWS[j], COLS[j]), BF16) for j in range(3)],
            [vmem((COLS[j], RANK), F32) for j in range(3)],
            [vmem((ROWS[j], COLS[j]), F32) for j in range(3)],
            [vmem((3 * PADDED[j], 2 * RANK), BF16) for j in range(3)],
            dma((3,)),
            dma((3, 4)),
        ],
        compiler_params=pltpu.CompilerParams(vmem_limit_bytes=44 * 2**20),
        name="update",
    )(weight, factor, buffer, basis, squares)
    pick = lambda group: (group[1], group[2], group[0])
    return (*pick(moment), *pick(weight), *pick(right), *pick(change))


def solution(mesh):
    matrix, factor = P(("fsdp", "rep"), "tp"), P("tp", None)
    in_specs = (matrix, matrix, matrix, factor) * 3
    out_specs = (matrix,) * 6 + (factor,) * 3 + (matrix,) * 3
    return jax.shard_map(local, mesh=mesh, in_specs=in_specs, out_specs=out_specs, check_vma=False)
```

```python
import functools
import math

import jax
import jax.numpy as jnp
from jax import lax
from jax.experimental import pallas as pl
from jax.experimental.pallas import tpu as pltpu
from jax.sharding import PartitionSpec as P

ROWS = (216, 80, 80)
PADDED = (224, 80, 80)
COLS = (2560, 2560, 6912)
UNITS = (5, 5, 14)
SPANS = ((1280, 1280), (1280, 1280), (2304, 2304, 2304))
SHAPE = ((13824, 5120), (5120, 5120), (5120, 13824))
UNIT = 512
RANK = 128
DECAY = 0.95
LEARN_RATE = 0.02
EPSILON = 1e-08
MESH = pl.DeviceIdType.MESH
F32 = jnp.float32
BF16 = jnp.bfloat16
HIGHEST = lax.Precision.HIGHEST
AXES = ((0, 1, 2), (1, 2, 0), (2, 0, 1))
TERMS = tuple(3 * rows + (-3 * rows) % 128 for rows in PADDED)

PER_PART = (3, 3, 2)


def make_parts():
    units = [(matrix, unit) for matrix in range(3) for unit in range(UNITS[matrix])]
    parts = []
    for count in PER_PART:
        for _ in range(3):
            parts.append(units[:count])
            units = units[count:]
    return parts


PARTS = make_parts()
N_PARTS = len(PARTS)
GROUPS = ((1, (0, 1)), (1, (2, 3)), (1, (4,)), (0, (0, 1)), (0, (2, 3)), (0, (4,))) + tuple(
    (2, (unit, unit + 1)) for unit in range(0, 14, 2)
)
PLAN = (
    ("left", 0),
    ("left", 1),
    ("R1a", 0),
    ("left", 2),
    ("R1a", 1),
    ("gram", 0),
    ("R1b", 0),
    ("R1a", 2),
    ("gram", 1),
    ("R1b", 1),
    ("R1c", 0),
    ("R1b", 2),
    ("gram", 2),
    ("R1c", 1),
    ("R2b", 0),
    ("gram", 3),
    ("R1c", 2),
    ("R2b", 1),
    ("R2c", 0),
    ("R2b", 2),
    ("gram", 4),
    ("R2c", 1),
    ("gram", 5),
    ("chol", 0),
    ("R3c", 0),
    ("R2c", 2),
    ("chol", 1),
    ("chol", 2),
    ("R3c", 1),
    ("chol", 3),
    ("G3c", 0),
    ("chol", 4),
    ("R3c", 2),
    ("chol", 5),
    ("G3c", 1),
    ("G2b", 0),
    ("chol", 6),
    ("chol", 7),
    ("G3c", 2),
    ("G2b", 1),
    ("G2c", 0),
    ("G2b", 2),
    ("G2c", 1),
    ("G1b", 0),
    ("G2c", 2),
    ("G1b", 1),
    ("G1b", 2),
    ("G1c", 0),
    ("G1c", 1),
    ("G1c", 2),
)
HEIGHT = [8 * len(part) for part in PARTS]


def split(value):
    high = value.astype(BF16)
    return high, (value - high.astype(F32)).astype(BF16)


def nt_dot(first, second, precision=None):
    return lax.dot_general(first, second, (((1,), (1,)), ((), ())), precision=precision, preferred_element_type=F32)


def tn_dot(first, second, precision=None):
    return lax.dot_general(first, second, (((0,), (0,)), ((), ())), precision=precision, preferred_element_type=F32)


def each(count, body):
    def step(index, carry):
        body(index)
        return carry

    lax.fori_loop(0, count, step, 0)


def reduce_kernel(
    momentum,
    gradient,
    right,
    weight,
    factor,
    buffer,
    basis,
    squares,
    weight_in,
    partial,
    summed,
    inbox1,
    inbox2,
    inbox3,
    pairs,
    grad_in,
    right_in,
    terms,
    left,
    left_in,
    left_terms,
    gram,
    gram_in1,
    gram_in2,
    gram_in3,
    gram_sum,
    gram_all,
    matrix,
    inverse,
    inverse_terms,
    squares_in,
    load_sem,
    send_sem,
    recv_sem,
    misc_send,
    misc_recv,
):
    rows_at = lax.axis_index("fsdp")
    core = lax.axis_index("tp")
    coord = (lax.axis_index("rep"), rows_at % 4, rows_at // 4)

    def device(axis, shift):
        moved = [(coord[a] + shift) % 4 if a == axis else coord[a] for a in range(3)]
        return (moved[2] * 4 + moved[1], core, moved[0])

    partner = (rows_at, 1 - core, coord[0])

    loads = []
    for j in range(3):
        steps = []
        start = 0
        for s, span in enumerate(SPANS[j]):
            cols = pl.ds(start, span)
            copies = [
                pltpu.make_async_copy(momentum[j].at[:, cols], buffer[j].at[:, cols], load_sem.at[j, s, 0]),
                pltpu.make_async_copy(gradient[j].at[:, cols], grad_in[j].at[:, cols], load_sem.at[j, s, 1]),
                pltpu.make_async_copy(right[j].at[cols, :], right_in[j].at[cols, :], load_sem.at[j, s, 2]),
            ]
            for copy in copies:
                copy.start()
            steps.append((start, span, copies))
            start += span
        loads.append(steps)

    weight_loads = [pltpu.make_async_copy(weight[j], weight_in[j], load_sem.at[j, 3, 0]) for j in range(3)]
    for copy in weight_loads:
        copy.start()

    barrier = pltpu.get_barrier_semaphore()
    peers = [device(axis, shift) for axis in range(3) for shift in (1, 2, 3)] + [partner]
    for peer in peers:
        pl.semaphore_signal(barrier, inc=1, device_id=peer, device_id_type=MESH)

    started = []

    def send(first, second, src, dst, target):
        copy = pltpu.make_async_remote_copy(
            src_ref=src, dst_ref=dst, send_sem=first, recv_sem=second, device_id=target, device_id_type=MESH
        )
        copy.start()
        return copy

    def misc(index, src, dst, target):
        copy = send(misc_send.at[index], misc_recv.at[index], src, dst, target)
        started.append(copy)
        return copy

    def wait_all(ref, sem):
        pltpu.make_async_copy(ref, ref, sem).wait()

    held = {}

    def left_partial(j):
        pad = PADDED[j]
        total = None
        for start, span, copies in loads[j]:
            for copy in copies:
                copy.wait()

            def prepare(i, start=start):
                cols = pl.ds(pl.multiple_of(start + i * 256, 256), 256)
                value = buffer[j][:, cols] + grad_in[j][:, cols].astype(F32)
                buffer[j][:, cols] = value
                if pad > ROWS[j]:
                    value = jnp.concatenate([value, jnp.zeros((pad - ROWS[j], 256), F32)], axis=0)
                high, low = split(value)
                terms[j][0:pad, cols] = high
                terms[j][pad : 2 * pad, cols] = low
                terms[j][2 * pad : 3 * pad, cols] = high

            each(span // 256, prepare)
            right_terms = jnp.concatenate(split(right_in[j][start : start + span, :]), axis=1)
            product = jnp.dot(terms[j][0 : 2 * pad, start : start + span], right_terms, preferred_element_type=F32)
            product = product[0:pad, 0:RANK] + (product[0:pad, RANK:] + product[pad:, 0:RANK])
            total = product if total is None else total + product
        left[j][...] = total
        if terms[j].shape[1] > COLS[j]:
            terms[j][:, COLS[j] :] = jnp.zeros((3 * pad, terms[j].shape[1] - COLS[j]), BF16)
        return misc(j, left[j], left_in[j], partner)

    def left_finish(j, copy):
        copy.wait_recv()
        pad = PADDED[j]
        value = left[j][...] + left_in[j][...]
        left_in[j][...] = value
        high = value.astype(BF16).astype(F32)
        low = value - high
        pieces = [high, high, low]
        if TERMS[j] > 3 * pad:
            pieces.append(jnp.zeros((TERMS[j] - 3 * pad, RANK), F32))
        left_terms[j][...] = jnp.concatenate(pieces, axis=0).T.astype(BF16)

    def gram_partial(j):
        value = left_in[j][...]
        result = tn_dot(value, value, HIGHEST)
        gram[:, :, j] = result.reshape(2, 4, 16, RANK)

    def factor_unit(k, slot):
        j, unit = PARTS[k][slot]
        cols = slice(unit * UNIT, (unit + 1) * UNIT)
        product = jnp.dot(left_terms[j][:, 0 : 3 * PADDED[j]], terms[j][:, cols], preferred_element_type=F32)
        partial[k][:, slot * 8 : slot * 8 + 8, :] = product.T.reshape(64, 8, RANK)

    finished = set()

    def finish(j):
        if j not in finished:
            finished.add(j)
            left_finish(j, held["left", j])

    def factor_part(k):
        for j in sorted({j for j, _ in PARTS[k]}):
            finish(j)
        for slot in range(len(PARTS[k])):
            factor_unit(k, slot)

    def place(ref, base, half, chunk, side):
        return ref.at[pl.ds(base + ((chunk % 4) * 2 + side) * half, half)]

    def first_coord(k):
        return coord[AXES[k % 3][0]]

    def reduce_setting(k, phase):
        axis = AXES[k % 3][phase - 1]
        base, half, inbox = (0, 8, inbox1[k]) if phase == 1 else (16 * first_coord(k), 2, inbox2[k])
        at = functools.partial(place, partial[k], base, half)

        def out(n, ref, box, shift):
            sem = recv_sem.at[k, 3 * (phase - 1) + min(n, 2)]
            send(send_sem.at[k, 0], sem, ref, inbox.at[box], device(axis, shift))

        return coord[axis], at, half, inbox, out

    def reduce_start(k, phase):
        i, at, half, inbox, out = reduce_setting(k, phase)
        out(0, at(i + 2, 0), 0, 1)
        out(1, at(i + 2, 1), 1, 3)
        out(2, at(i + 1, 1), 2, 1)
        out(2, at(i + 3, 0), 3, 3)

    def reduce_relay(k, phase):
        i, at, half, inbox, out = reduce_setting(k, phase)
        for side, chunk, shift in ((0, i + 1, 1), (1, i + 3, 3)):
            wait_all(inbox.at[side], recv_sem.at[k, 3 * (phase - 1) + side])
            ref = at(chunk, side)
            ref[...] += inbox[side]
            out(2, ref, 4 + side, shift)

    def reduce_finish(k, phase):
        i, at, half, inbox, out = reduce_setting(k, phase)
        wait_all(inbox.at[2:6], recv_sem.at[k, 3 * (phase - 1) + 2])
        for side, near, relayed in ((0, 3, 4), (1, 2, 5)):
            at(i, side)[...] += inbox[near] + inbox[relayed]

    def exchange_setting(k):
        axes = AXES[k % 3]
        second, third = coord[axes[1]], coord[axes[2]]
        shifts = (1 + 2 * (third % 2), 3 - 2 * (third % 2))
        return axes[2], shifts, pl.ds(16 * coord[axes[0]] + 4 * second, 4), pl.ds(4 * second, 4)

    def exchange_start(k):
        axis, shifts, mine, _ = exchange_setting(k)
        send(send_sem.at[k, 2], recv_sem.at[k, 6], partial[k].at[mine], inbox3[k].at[0], device(axis, shifts[0]))

    def exchange_middle(k):
        axis, shifts, mine, _ = exchange_setting(k)
        wait_all(inbox3[k].at[0], recv_sem.at[k, 6])
        pairs[k][...] = partial[k][mine] + inbox3[k][0]
        send(send_sem.at[k, 3], recv_sem.at[k, 7], pairs[k], inbox3[k].at[1], device(axis, shifts[1]))

    def exchange_finish(k):
        _, _, _, there = exchange_setting(k)
        wait_all(inbox3[k].at[1], recv_sem.at[k, 7])
        summed[k][there] = pairs[k][...] + inbox3[k][1]

    def gather_setting(k, phase):
        axis = AXES[k % 3][phase - 1]
        ref, half, first = (factor[k], 8, 11) if phase == 1 else (summed[k], 2, 8)
        at = functools.partial(place, ref, 0, half)

        def out(n, there, shift):
            send(send_sem.at[k, 1], recv_sem.at[k, first + n], there, there, device(axis, shift))

        def arrived(n):
            wait_all(ref.at[0:half] if n < 2 else ref.at[0 : 4 * half], recv_sem.at[k, first + n])

        return coord[axis], at, out, arrived

    def gather_start(k, phase):
        i, at, out, arrived = gather_setting(k, phase)
        out(0, at(i, 0), 1)
        out(1, at(i, 1), 3)
        out(2, at(i, 1), 1)
        out(2, at(i, 0), 3)

    def gather_relay(k, phase):
        i, at, out, arrived = gather_setting(k, phase)
        arrived(0)
        out(2, at(i + 3, 0), 1)
        arrived(1)
        out(2, at(i + 1, 1), 3)

    def gather_finish(k, phase):
        gather_setting(k, phase)[3](2)

    def apply_inverse(k):
        base = 16 * first_coord(k)
        for j in range(3):
            slots = [slot for slot, (other, _) in enumerate(PARTS[k]) if other == j]
            if not slots:
                continue
            rows = slice(slots[0] * 8, slots[-1] * 8 + 8)
            count = 8 * len(slots)
            high, low = split(summed[k][:, rows, :].reshape(16 * count, RANK))
            product = nt_dot(jnp.concatenate([high, low], axis=0), inverse_terms[j])
            product = product[: 16 * count, :RANK] + (product[: 16 * count, RANK:] + product[16 * count :, :RANK])
            factor[k][pl.ds(base, 16), rows, :] = product.reshape(16, count, RANK)

    def gram_scatter():
        x = coord[0]
        return [
            misc(2 + s, gram.at[core, (x + s) % 4], gram_in1.at[x], device(0, s)) for s in (1, 2, 3)
        ]

    def gram_exchange(copies, own_value, box, sent, axis, n):
        for copy in copies:
            copy.wait_recv()
        box_before, at_before = own_value
        box_before[at_before] = sent[0][...]
        sent[1][...] = (box_before[0] + box_before[1]) + (box_before[2] + box_before[3])
        return [misc(n + s, sent[1], box.at[coord[axis]], device(axis, s)) for s in (1, 2, 3)]

    def gram_gather(copies):
        x = coord[0]
        for copy in copies:
            copy.wait_recv()
        gram_in3[coord[2]] = gram_sum[1]
        ref = gram_all.at[core, x]
        ref[...] = (gram_in3[0] + gram_in3[1]) + (gram_in3[2] + gram_in3[3])
        return [misc(11 + s, ref, ref, device(0, s)) for s in (1, 2, 3)]

    def gram_swap(copies):
        for copy in copies:
            copy.wait_recv()
        return misc(15, gram_all.at[core], gram_all.at[core], partner)

    def gram_finish(copy):
        copy.wait_recv()
        row = lax.broadcasted_iota(jnp.int32, (RANK, RANK), 0)
        col = lax.broadcasted_iota(jnp.int32, (RANK, RANK), 1)
        for j in range(3):
            matrix[j, :, 0:RANK] = gram_all[:, :, j].reshape(RANK, RANK)
            matrix[j, :, RANK:] = (row == col).astype(F32)

    def eliminate(piece):
        first, start = piece // 4 * 32, piece * 8
        stop = first + 32
        count = stop - start
        a = matrix[:, start:stop, 0:RANK]
        x = matrix[:, start:stop, RANK:]
        rows = lax.broadcasted_iota(jnp.int32, (3, count, RANK), 1)
        columns = [jnp.broadcast_to(a[:, :, start + n : start + n + 1], (3, count, RANK)) for n in range(8)]
        pivots = []
        for n in range(8):
            pivot = columns[n][:, n : n + 1, :]
            pivots.append(pivot)
            scale = 1.0 / jnp.broadcast_to(pivot, (3, 8, RANK))
            ratio = jnp.where(rows > n, columns[n] * scale[:, 0:1, :], 0.0)
            for later in range(n + 1, 8):
                columns[later] = columns[later] - ratio * columns[later][:, n : n + 1, :]
            a = a - ratio * a[:, n : n + 1, :]
            x = x - ratio * x[:, n : n + 1, :]
        scale = 1.0 / jnp.sqrt(jnp.concatenate(pivots, axis=1))
        matrix[:, start : start + 8, 0:RANK] = a[:, 0:8] * scale
        inverse[:, start : start + 8, :] = x[:, 0:8] * scale
        if count > 8:
            matrix[:, start + 8 : stop, 0:RANK] = a[:, 8:]
            matrix[:, start + 8 : stop, RANK:] = x[:, 8:]
        elif stop < RANK:
            lane = lax.broadcasted_iota(jnp.int32, (32, RANK), 1)
            for j in range(3):
                panel = jnp.where(lane >= stop, matrix[j, first:stop, 0:RANK], 0.0)
                both = jnp.concatenate([panel, inverse[j, first:stop, :]], axis=1)
                matrix[j, stop:] = matrix[j, stop:] - tn_dot(panel, both, HIGHEST)[stop:]
        else:
            for j in range(3):
                high, low = split(inverse[j])
                inverse_terms[j, 0:RANK] = high
                inverse_terms[j, RANK:] = low

    def basis_all():
        for j in range(3):
            basis[j][...] = nt_dot(left_in[j][...], inverse[j], HIGHEST)[0 : ROWS[j]]

    sums = [jnp.zeros((8, RANK), F32) for _ in range(3)]

    def add_squares(k):
        for slot, (j, _) in enumerate(PARTS[k]):
            total = None
            for start in range(0, 64, 8):
                value = factor[k][start : start + 8, slot * 8 : slot * 8 + 8, :]
                total = value * value if total is None else total + value * value
            sums[j] = sums[j] + jnp.sum(total, axis=0)

    def run(name, value):
        parts = range(3 * value, 3 * value + 3)
        if name == "left":
            held["left", value] = left_partial(value)
        elif name == "gram":
            if value == 0:
                for j in range(3):
                    finish(j)
                    gram_partial(j)
                held["gram"] = gram_scatter()
            elif value == 1:
                sent = (gram.at[core, coord[0]], gram_sum.at[0])
                held["gram"] = gram_exchange(held["gram"], (gram_in1, coord[0]), gram_in2, sent, 1, 5)
            elif value == 2:
                sent = (gram_sum.at[0], gram_sum.at[1])
                held["gram"] = gram_exchange(held["gram"], (gram_in2, coord[1]), gram_in3, sent, 2, 8)
            elif value == 3:
                held["gram"] = gram_gather(held["gram"])
            elif value == 4:
                held["gram"] = gram_swap(held["gram"])
            else:
                gram_finish(held["gram"])
        elif name == "chol":
            for piece in range(2 * value, 2 * value + 2):
                eliminate(piece)
            if value == 7:
                basis_all()
        for k in parts:
            if name == "R1a":
                factor_part(k)
                reduce_start(k, 1)
            elif name == "R1b":
                reduce_relay(k, 1)
            elif name == "R1c":
                reduce_finish(k, 1)
                reduce_start(k, 2)
            elif name == "R2b":
                reduce_relay(k, 2)
            elif name == "R2c":
                reduce_finish(k, 2)
                exchange_start(k)
            elif name == "R3c":
                exchange_middle(k)
            elif name == "G3c":
                exchange_finish(k)
                gather_start(k, 2)
            elif name == "G2b":
                gather_relay(k, 2)
            elif name == "G2c":
                gather_finish(k, 2)
                apply_inverse(k)
                gather_start(k, 1)
            elif name == "G1b":
                gather_relay(k, 1)
            elif name == "G1c":
                gather_finish(k, 1)
                add_squares(k)

    pl.semaphore_wait(barrier, len(peers))
    for name, value in PLAN:
        run(name, value)
    rows = [jnp.sum(value, axis=0, keepdims=True) for value in sums]
    squares_in[0] = jnp.concatenate(rows + [jnp.zeros((5, RANK), F32)], axis=0)
    copy = misc(16, squares_in.at[0], squares_in.at[1], partner)
    for load in weight_loads:
        load.wait()
    for k in range(N_PARTS):
        wait_all(partial[k].at[0:60], send_sem.at[k, 0])
        wait_all(pairs[k], send_sem.at[k, 2])
        wait_all(pairs[k], send_sem.at[k, 3])
        wait_all(partial[k].at[0:60], send_sem.at[k, 1])
    copy.wait_recv()
    squares[...] = squares_in[0] + squares_in[1]
    for copy in started:
        copy.wait_send()


def update_kernel(
    weight_in,
    factor,
    buffer,
    basis,
    squares,
    moment_out,
    weight_out,
    right_out,
    change_out,
    moment_box,
    weight_box,
    right_box,
    change_box,
    rows_in,
    store_sem,
):
    scale = 1.0 / (jnp.sqrt(squares[...]) + EPSILON)
    for j in range(3):
        rows, pad = ROWS[j], PADDED[j]
        value = basis[j][...]
        if pad > rows:
            value = jnp.concatenate([value, jnp.zeros((pad - rows, RANK), F32)], axis=0)
        step_size = LEARN_RATE * math.sqrt(SHAPE[j][0] / SHAPE[j][1])
        high, low = split(value * (scale[j : j + 1] * step_size))
        rows_in[j][0:pad, 0:RANK] = high
        rows_in[j][0:pad, RANK:] = high
        rows_in[j][pad : 2 * pad, 0:RANK] = low
        rows_in[j][pad : 2 * pad, RANK:] = jnp.zeros((pad, RANK), BF16)
        moment = (value * (1.0 - DECAY)).astype(BF16)
        rows_in[j][2 * pad :, 0:RANK] = moment
        rows_in[j][2 * pad :, RANK:] = jnp.zeros((pad, RANK), BF16)
    where = {unit: (k, slot) for k, part in enumerate(PARTS) for slot, unit in enumerate(part)}
    for j, units in GROUPS:
        rows, pad = ROWS[j], PADDED[j]
        for unit in units:
            k, slot = where[j, unit]
            start = unit * UNIT
            width = min(UNIT, COLS[j] - start)
            value = factor[k][0 : width // 8, slot * 8 : slot * 8 + 8, :].reshape(width, RANK)
            cols = slice(start, start + width)
            right_box[j][cols, :] = value * scale[j : j + 1]
            high, low = split(value)
            product = nt_dot(rows_in[j][...], jnp.concatenate([high, low], axis=1))
            change = product[0:rows] + product[pad : pad + rows]
            change_box[j][:, cols] = change
            moment_box[j][:, cols] = buffer[j][:, cols] - product[2 * pad : 2 * pad + rows]
            weight_box[j][:, cols] = (weight_in[j][:, cols].astype(F32) - change).astype(BF16)
        cols = slice(units[0] * UNIT, min(units[-1] * UNIT + UNIT, COLS[j]))
        pltpu.make_async_copy(right_box[j].at[cols, :], right_out[j].at[cols, :], store_sem.at[j, 0]).start()
        for n, (box, out) in enumerate(((change_box, change_out), (moment_box, moment_out), (weight_box, weight_out))):
            pltpu.make_async_copy(box[j].at[:, cols], out[j].at[:, cols], store_sem.at[j, n + 1]).start()
    for j in range(3):
        for n, (box, out) in enumerate(
            ((right_box, right_out), (change_box, change_out), (moment_box, moment_out), (weight_box, weight_out))
        ):
            pltpu.make_async_copy(box[j], out[j], store_sem.at[j, n]).wait()


def local(
    out_momentum,
    out_gradient,
    out_weight,
    out_right,
    up_momentum,
    up_gradient,
    up_weight,
    up_right,
    down_momentum,
    down_gradient,
    down_weight,
    down_right,
):
    momentum = [down_momentum, out_momentum, up_momentum]
    gradient = [down_gradient, out_gradient, up_gradient]
    weight = [down_weight, out_weight, up_weight]
    right = [down_right, out_right, up_right]
    vmem = pltpu.VMEM
    anywhere = pl.BlockSpec(memory_space=pl.ANY)
    inside = pl.BlockSpec(memory_space=vmem)
    dma = pltpu.SemaphoreType.DMA
    each_part = lambda lead: [vmem((*lead, HEIGHT[k], RANK), F32) for k in range(N_PARTS)]

    factor_shapes = [jax.ShapeDtypeStruct((64, HEIGHT[k], RANK), F32) for k in range(N_PARTS)]
    buffer_shapes = [jax.ShapeDtypeStruct((ROWS[j], COLS[j]), F32) for j in range(3)]
    basis_shapes = [jax.ShapeDtypeStruct((ROWS[j], RANK), F32) for j in range(3)]
    weight_shapes = [jax.ShapeDtypeStruct((ROWS[j], COLS[j]), BF16) for j in range(3)]
    middle = [factor_shapes, buffer_shapes, basis_shapes, jax.ShapeDtypeStruct((8, RANK), F32), weight_shapes]
    placed = jax.tree.map(lambda s: vmem(s.shape, s.dtype), middle)
    terms_cols = [UNIT * count for count in UNITS]
    middle = pl.pallas_call(
        reduce_kernel,
        out_shape=placed,
        in_specs=[[anywhere] * 3] * 4,
        out_specs=jax.tree.map(lambda s: inside, middle),
        scratch_shapes=[
            each_part((64,)),
            each_part((16,)),
            each_part((6, 8)),
            each_part((6, 2)),
            each_part((2, 4)),
            each_part((4,)),
            [vmem((ROWS[j], COLS[j]), BF16) for j in range(3)],
            [vmem((COLS[j], RANK), F32) for j in range(3)],
            [vmem((3 * PADDED[j], terms_cols[j]), BF16) for j in range(3)],
            [vmem((PADDED[j], RANK), F32) for j in range(3)],
            [vmem((PADDED[j], RANK), F32) for j in range(3)],
            [vmem((RANK, TERMS[j]), BF16) for j in range(3)],
            vmem((2, 4, 3, 16, RANK), F32),
            vmem((4, 3, 16, RANK), F32),
            vmem((4, 3, 16, RANK), F32),
            vmem((4, 3, 16, RANK), F32),
            vmem((2, 3, 16, RANK), F32),
            vmem((2, 4, 3, 16, RANK), F32),
            vmem((3, RANK, 2 * RANK), F32),
            vmem((3, RANK, RANK), F32),
            vmem((3, 2 * RANK, RANK), BF16),
            vmem((2, 8, RANK), F32),
            dma((3, 4, 3)),
            dma((N_PARTS, 4)),
            dma((N_PARTS, 14)),
            dma((17,)),
            dma((17,)),
        ],
        compiler_params=pltpu.CompilerParams(
            collective_id=0, has_side_effects=True, vmem_limit_bytes=45 * 2**20
        ),
        name="reduce",
    )(momentum, gradient, right, weight)
    keep = lambda x: pltpu.with_memory_space_constraint(x, vmem)
    factor, buffer, basis, squares, weight = jax.tree.map(keep, tuple(middle))
    matrices = lambda dtype: [jax.ShapeDtypeStruct((ROWS[j], COLS[j]), dtype) for j in range(3)]
    factors = [jax.ShapeDtypeStruct((COLS[j], RANK), F32) for j in range(3)]
    results = [matrices(F32), matrices(BF16), factors, matrices(F32)]
    moment, weight, right, change = pl.pallas_call(
        update_kernel,
        out_shape=results,
        in_specs=[[inside] * 3, [inside] * N_PARTS, [inside] * 3, [inside] * 3, inside],
        out_specs=jax.tree.map(lambda s: anywhere, results),
        scratch_shapes=[
            [vmem((ROWS[j], COLS[j]), F32) for j in range(3)],
            [vmem((ROWS[j], COLS[j]), BF16) for j in range(3)],
            [vmem((COLS[j], RANK), F32) for j in range(3)],
            [vmem((ROWS[j], COLS[j]), F32) for j in range(3)],
            [vmem((3 * PADDED[j], 2 * RANK), BF16) for j in range(3)],
            dma((3, 4)),
        ],
        compiler_params=pltpu.CompilerParams(vmem_limit_bytes=40 * 2**20),
        name="update",
    )(weight, factor, buffer, basis, squares)
    pick = lambda group: (group[1], group[2], group[0])
    return (*pick(moment), *pick(weight), *pick(right), *pick(change))


def solution(mesh):
    matrix, factor = P(("fsdp", "rep"), "tp"), P("tp", None)
    in_specs = (matrix, matrix, matrix, factor) * 3
    out_specs = (matrix,) * 6 + (factor,) * 3 + (matrix,) * 3
    return jax.shard_map(local, mesh=mesh, in_specs=in_specs, out_specs=out_specs, check_vma=False)
```

```python
import functools
import math

import jax
import jax.numpy as jnp
from jax import lax
from jax.experimental import pallas as pl
from jax.experimental.pallas import tpu as pltpu
from jax.sharding import PartitionSpec as P

ROWS = (216, 80, 80)
PADDED = (224, 80, 80)
COLS = (2560, 2560, 6912)
UNITS = (5, 5, 14)
SPANS = ((1280, 1280), (1280, 1280), (2304, 2304, 2304))
SHAPE = ((13824, 5120), (5120, 5120), (5120, 13824))
UNIT = 512
RANK = 128
DECAY = 0.95
LEARN_RATE = 0.02
EPSILON = 1e-08
MESH = pl.DeviceIdType.MESH
F32 = jnp.float32
BF16 = jnp.bfloat16
HIGHEST = lax.Precision.HIGHEST
AXES = ((0, 1, 2), (1, 2, 0), (2, 0, 1))
TERMS = tuple(3 * rows + (-3 * rows) % 128 for rows in PADDED)

PER_PART = ((3, 3, 3), (3, 3, 3), (2, 2, 2))


def make_parts():
    units = [(matrix, unit) for matrix in range(3) for unit in range(UNITS[matrix])]
    parts = []
    for count in sum(PER_PART, ()):
        parts.append(units[:count])
        units = units[count:]
    return parts


PARTS = make_parts()
N_PARTS = len(PARTS)
GROUPS = ((1, (0, 1)), (1, (2, 3)), (1, (4,)), (0, (0, 1)), (0, (2, 3)), (0, (4,))) + tuple(
    (2, (unit, unit + 1)) for unit in range(0, 14, 2)
)
PLAN = (
    ("left", 0),
    ("left", 1),
    ("R1a", 0),
    ("left", 2),
    ("R1b", 0),
    ("gram", 0),
    ("R1a", 1),
    ("gram", 1),
    ("R1c", 0),
    ("R1b", 1),
    ("R1a", 2),
    ("gram", 2),
    ("R2b", 0),
    ("R1c", 1),
    ("R1b", 2),
    ("gram", 3),
    ("R2c", 0),
    ("R2b", 1),
    ("R1c", 2),
    ("R3c", 0),
    ("gram", 4),
    ("R2c", 1),
    ("gram", 5),
    ("chol", 0),
    ("R2b", 2),
    ("chol", 1),
    ("G3c", 0),
    ("chol", 2),
    ("R3c", 1),
    ("chol", 3),
    ("R2c", 2),
    ("chol", 4),
    ("G2b", 0),
    ("chol", 5),
    ("chol", 6),
    ("G3c", 1),
    ("chol", 7),
    ("R3c", 2),
    ("G2c", 0),
    ("G2b", 1),
    ("G3c", 2),
    ("G1b", 0),
    ("G2b", 2),
    ("G2c", 1),
    ("G2c", 2),
    ("G1b", 1),
    ("G1c", 0),
    ("G1b", 2),
    ("norms", 0),
    ("sent", 0),
    ("G1c", 1),
    ("norms", 1),
    ("G1c", 2),
)
HEIGHT = [8 * len(part) for part in PARTS]


def split(value):
    high = value.astype(BF16)
    return high, (value - high.astype(F32)).astype(BF16)


def nt_dot(first, second, precision=None):
    return lax.dot_general(first, second, (((1,), (1,)), ((), ())), precision=precision, preferred_element_type=F32)


def tn_dot(first, second, precision=None):
    return lax.dot_general(first, second, (((0,), (0,)), ((), ())), precision=precision, preferred_element_type=F32)


def each(count, body):
    def step(index, carry):
        body(index)
        return carry

    lax.fori_loop(0, count, step, 0)


def reduce_kernel(
    momentum,
    gradient,
    right,
    weight,
    factor,
    buffer,
    rows_out,
    squares,
    weight_in,
    partial,
    summed,
    inbox1,
    inbox2,
    inbox3,
    pairs,
    grad_in,
    right_in,
    terms,
    left,
    left_in,
    left_terms,
    gram,
    gram_in1,
    gram_in2,
    gram_in3,
    gram_sum,
    gram_all,
    matrix,
    inverse,
    inverse_terms,
    basis,
    norms,
    squares_in,
    load_sem,
    send_sem,
    recv_sem,
    misc_send,
    misc_recv,
    norm_send,
    norm_recv,
):
    rows_at = lax.axis_index("fsdp")
    core = lax.axis_index("tp")
    coord = (lax.axis_index("rep"), rows_at % 4, rows_at // 4)

    def device(axis, shift):
        moved = [(coord[a] + shift) % 4 if a == axis else coord[a] for a in range(3)]
        return (moved[2] * 4 + moved[1], core, moved[0])

    partner = (rows_at, 1 - core, coord[0])

    loads = []
    for j in range(3):
        steps = []
        start = 0
        for s, span in enumerate(SPANS[j]):
            cols = pl.ds(start, span)
            copies = [
                pltpu.make_async_copy(momentum[j].at[:, cols], buffer[j].at[:, cols], load_sem.at[j, s, 0]),
                pltpu.make_async_copy(gradient[j].at[:, cols], grad_in[j].at[:, cols], load_sem.at[j, s, 1]),
                pltpu.make_async_copy(right[j].at[cols, :], right_in[j].at[cols, :], load_sem.at[j, s, 2]),
            ]
            for copy in copies:
                copy.start()
            steps.append((start, span, copies))
            start += span
        loads.append(steps)

    weight_loads = [pltpu.make_async_copy(weight[j], weight_in[j], load_sem.at[j, 3, 0]) for j in range(3)]
    for copy in weight_loads:
        copy.start()

    barrier = pltpu.get_barrier_semaphore()
    peers = [device(axis, shift) for axis in range(3) for shift in (1, 2, 3)] + [partner]
    for peer in peers:
        pl.semaphore_signal(barrier, inc=1, device_id=peer, device_id_type=MESH)

    started = []

    def send(first, second, src, dst, target):
        copy = pltpu.make_async_remote_copy(
            src_ref=src, dst_ref=dst, send_sem=first, recv_sem=second, device_id=target, device_id_type=MESH
        )
        copy.start()
        return copy

    def misc(index, src, dst, target):
        copy = send(misc_send.at[index], misc_recv.at[index], src, dst, target)
        started.append(copy)
        return copy

    def wait_all(ref, sem):
        pltpu.make_async_copy(ref, ref, sem).wait()

    held = {}

    def left_partial(j):
        pad = PADDED[j]
        total = None
        for start, span, copies in loads[j]:
            for copy in copies:
                copy.wait()

            def prepare(i, start=start):
                cols = pl.ds(pl.multiple_of(start + i * 256, 256), 256)
                value = buffer[j][:, cols] + grad_in[j][:, cols].astype(F32)
                buffer[j][:, cols] = value
                if pad > ROWS[j]:
                    value = jnp.concatenate([value, jnp.zeros((pad - ROWS[j], 256), F32)], axis=0)
                high, low = split(value)
                terms[j][0:pad, cols] = high
                terms[j][pad : 2 * pad, cols] = low
                terms[j][2 * pad : 3 * pad, cols] = high

            each(span // 256, prepare)
            right_terms = jnp.concatenate(split(right_in[j][start : start + span, :]), axis=1)
            product = jnp.dot(terms[j][0 : 2 * pad, start : start + span], right_terms, preferred_element_type=F32)
            product = product[0:pad, 0:RANK] + (product[0:pad, RANK:] + product[pad:, 0:RANK])
            total = product if total is None else total + product
        left[j][...] = total
        if terms[j].shape[1] > COLS[j]:
            terms[j][:, COLS[j] :] = jnp.zeros((3 * pad, terms[j].shape[1] - COLS[j]), BF16)
        return misc(j, left[j], left_in[j], partner)

    def left_finish(j, copy):
        copy.wait_recv()
        pad = PADDED[j]
        value = left[j][...] + left_in[j][...]
        left_in[j][...] = value
        high = value.astype(BF16).astype(F32)
        low = value - high
        pieces = [high, high, low]
        if TERMS[j] > 3 * pad:
            pieces.append(jnp.zeros((TERMS[j] - 3 * pad, RANK), F32))
        left_terms[j][...] = jnp.concatenate(pieces, axis=0).T.astype(BF16)

    def gram_partial(j):
        value = left_in[j][...]
        result = tn_dot(value, value, HIGHEST)
        gram[:, :, j] = result.reshape(2, 4, 16, RANK)

    def factor_unit(k, slot):
        j, unit = PARTS[k][slot]
        cols = slice(unit * UNIT, (unit + 1) * UNIT)
        product = jnp.dot(left_terms[j][:, 0 : 3 * PADDED[j]], terms[j][:, cols], preferred_element_type=F32)
        partial[k][:, slot * 8 : slot * 8 + 8, :] = product.T.reshape(64, 8, RANK)

    finished = set()

    def finish(j):
        if j not in finished:
            finished.add(j)
            left_finish(j, held["left", j])

    def factor_part(k):
        for j in sorted({j for j, _ in PARTS[k]}):
            finish(j)
        for slot in range(len(PARTS[k])):
            factor_unit(k, slot)

    def place(ref, base, half, chunk, side):
        return ref.at[pl.ds(base + ((chunk % 4) * 2 + side) * half, half)]

    def first_coord(k):
        return coord[AXES[k % 3][0]]

    def reduce_setting(k, phase):
        axis = AXES[k % 3][phase - 1]
        base, half, inbox = (0, 8, inbox1[k]) if phase == 1 else (16 * first_coord(k), 2, inbox2[k])
        at = functools.partial(place, partial[k], base, half)

        def out(n, ref, box, shift):
            sem = recv_sem.at[k, 3 * (phase - 1) + min(n, 2)]
            send(send_sem.at[k, 0], sem, ref, inbox.at[box], device(axis, shift))

        return coord[axis], at, half, inbox, out

    def reduce_start(k, phase):
        i, at, half, inbox, out = reduce_setting(k, phase)
        out(0, at(i + 2, 0), 0, 1)
        out(1, at(i + 2, 1), 1, 3)
        out(2, at(i + 1, 1), 2, 1)
        out(2, at(i + 3, 0), 3, 3)

    def reduce_relay(k, phase):
        i, at, half, inbox, out = reduce_setting(k, phase)
        for side, chunk, shift in ((0, i + 1, 1), (1, i + 3, 3)):
            wait_all(inbox.at[side], recv_sem.at[k, 3 * (phase - 1) + side])
            ref = at(chunk, side)
            ref[...] += inbox[side]
            out(2, ref, 4 + side, shift)

    def reduce_finish(k, phase):
        i, at, half, inbox, out = reduce_setting(k, phase)
        wait_all(inbox.at[2:6], recv_sem.at[k, 3 * (phase - 1) + 2])
        for side, near, relayed in ((0, 3, 4), (1, 2, 5)):
            at(i, side)[...] += inbox[near] + inbox[relayed]

    def exchange_setting(k):
        axes = AXES[k % 3]
        second, third = coord[axes[1]], coord[axes[2]]
        shifts = (1 + 2 * (third % 2), 3 - 2 * (third % 2))
        return axes[2], shifts, pl.ds(16 * coord[axes[0]] + 4 * second, 4), pl.ds(4 * second, 4)

    def exchange_start(k):
        axis, shifts, mine, _ = exchange_setting(k)
        send(send_sem.at[k, 2], recv_sem.at[k, 6], partial[k].at[mine], inbox3[k].at[0], device(axis, shifts[0]))

    def exchange_middle(k):
        axis, shifts, mine, _ = exchange_setting(k)
        wait_all(inbox3[k].at[0], recv_sem.at[k, 6])
        pairs[k][...] = partial[k][mine] + inbox3[k][0]
        send(send_sem.at[k, 3], recv_sem.at[k, 7], pairs[k], inbox3[k].at[1], device(axis, shifts[1]))

    def exchange_finish(k):
        _, _, _, there = exchange_setting(k)
        wait_all(inbox3[k].at[1], recv_sem.at[k, 7])
        summed[k][there] = pairs[k][...] + inbox3[k][1]

    def gather_setting(k, phase):
        axis = AXES[k % 3][phase - 1]
        ref, half, first = (factor[k], 8, 11) if phase == 1 else (summed[k], 2, 8)
        at = functools.partial(place, ref, 0, half)

        def out(n, there, shift):
            send(send_sem.at[k, 1], recv_sem.at[k, first + n], there, there, device(axis, shift))

        def arrived(n):
            wait_all(ref.at[0:half] if n < 2 else ref.at[0 : 4 * half], recv_sem.at[k, first + n])

        return coord[axis], at, out, arrived

    def gather_start(k, phase):
        i, at, out, arrived = gather_setting(k, phase)
        out(0, at(i, 0), 1)
        out(1, at(i, 1), 3)
        out(2, at(i, 1), 1)
        out(2, at(i, 0), 3)

    def gather_relay(k, phase):
        i, at, out, arrived = gather_setting(k, phase)
        arrived(0)
        out(2, at(i + 3, 0), 1)
        arrived(1)
        out(2, at(i + 1, 1), 3)

    def gather_finish(k, phase):
        gather_setting(k, phase)[3](2)

    sums = [[jnp.zeros((8, RANK), F32) for _ in range(3)] for _ in range(3)]
    counted = [0] * 3

    def send_norms(part):
        axis = AXES[part][0]
        rows = [jnp.sum(value, axis=0, keepdims=True) for value in sums[part]]
        ref = norms.at[4 * part + coord[axis]]
        ref[...] = jnp.concatenate(rows + [jnp.zeros((5, RANK), F32)], axis=0)
        for shift in (1, 2, 3):
            send(norm_send.at[0], norm_recv.at[part], ref, ref, device(axis, shift))

    def swap_norms():
        total = None
        for part in range(3):
            wait_all(norms.at[0:3], norm_recv.at[part])
            n = 4 * part
            value = (norms[n] + norms[n + 1]) + (norms[n + 2] + norms[n + 3])
            total = value if total is None else total + value
        squares_in[0] = total
        held["norms"] = misc(16, squares_in.at[0], squares_in.at[1], partner)

    def finish_norms():
        held["norms"].wait_recv()
        total = squares_in[0] + squares_in[1]
        squares[...] = total
        scale = 1.0 / (jnp.sqrt(total) + EPSILON)
        for j in range(3):
            pad = PADDED[j]
            value = basis[j][...]
            step_size = LEARN_RATE * math.sqrt(SHAPE[j][0] / SHAPE[j][1])
            high, low = split(value * (scale[j : j + 1] * step_size))
            rows_out[j][0:pad, 0:RANK] = high
            rows_out[j][0:pad, RANK:] = high
            rows_out[j][pad : 2 * pad, 0:RANK] = low
            rows_out[j][pad : 2 * pad, RANK:] = jnp.zeros((pad, RANK), BF16)
            rows_out[j][2 * pad :, 0:RANK] = (value * (1.0 - DECAY)).astype(BF16)
            rows_out[j][2 * pad :, RANK:] = jnp.zeros((pad, RANK), BF16)

    def apply_inverse(k):
        base = 16 * first_coord(k)
        for j in range(3):
            slots = [slot for slot, (other, _) in enumerate(PARTS[k]) if other == j]
            if not slots:
                continue
            rows = slice(slots[0] * 8, slots[-1] * 8 + 8)
            count = 8 * len(slots)
            high, low = split(summed[k][:, rows, :].reshape(16 * count, RANK))
            product = nt_dot(jnp.concatenate([high, low], axis=0), inverse_terms[j])
            product = product[: 16 * count, :RANK] + (product[: 16 * count, RANK:] + product[16 * count :, :RANK])
            factor[k][pl.ds(base, 16), rows, :] = product.reshape(16, count, RANK)
            total = jnp.sum((product * product).reshape(2 * count, 8, RANK), axis=0)
            sums[k % 3][j] = sums[k % 3][j] + total
        counted[k % 3] += 1
        if counted[k % 3] == N_PARTS // 3:
            send_norms(k % 3)

    def gram_scatter():
        x = coord[0]
        return [
            misc(2 + s, gram.at[core, (x + s) % 4], gram_in1.at[x], device(0, s)) for s in (1, 2, 3)
        ]

    def gram_exchange(copies, own_value, box, sent, axis, n):
        for copy in copies:
            copy.wait_recv()
        box_before, at_before = own_value
        box_before[at_before] = sent[0][...]
        sent[1][...] = (box_before[0] + box_before[1]) + (box_before[2] + box_before[3])
        return [misc(n + s, sent[1], box.at[coord[axis]], device(axis, s)) for s in (1, 2, 3)]

    def gram_gather(copies):
        x = coord[0]
        for copy in copies:
            copy.wait_recv()
        gram_in3[coord[2]] = gram_sum[1]
        ref = gram_all.at[core, x]
        ref[...] = (gram_in3[0] + gram_in3[1]) + (gram_in3[2] + gram_in3[3])
        return [misc(11 + s, ref, ref, device(0, s)) for s in (1, 2, 3)]

    def gram_swap(copies):
        for copy in copies:
            copy.wait_recv()
        return misc(15, gram_all.at[core], gram_all.at[core], partner)

    def gram_finish(copy):
        copy.wait_recv()
        row = lax.broadcasted_iota(jnp.int32, (RANK, RANK), 0)
        col = lax.broadcasted_iota(jnp.int32, (RANK, RANK), 1)
        for j in range(3):
            matrix[j, :, 0:RANK] = gram_all[:, :, j].reshape(RANK, RANK)
            matrix[j, :, RANK:] = (row == col).astype(F32)

    def eliminate(piece):
        first, start = piece // 4 * 32, piece * 8
        stop = first + 32
        count = stop - start
        a = matrix[:, start:stop, 0:RANK]
        x = matrix[:, start:stop, RANK:]
        rows = lax.broadcasted_iota(jnp.int32, (3, count, RANK), 1)
        columns = [jnp.broadcast_to(a[:, :, start + n : start + n + 1], (3, count, RANK)) for n in range(8)]
        pivots = []
        for n in range(8):
            pivot = columns[n][:, n : n + 1, :]
            pivots.append(pivot)
            scale = 1.0 / jnp.broadcast_to(pivot, (3, 8, RANK))
            ratio = jnp.where(rows > n, columns[n] * scale[:, 0:1, :], 0.0)
            for later in range(n + 1, 8):
                columns[later] = columns[later] - ratio * columns[later][:, n : n + 1, :]
            a = a - ratio * a[:, n : n + 1, :]
            x = x - ratio * x[:, n : n + 1, :]
        scale = 1.0 / jnp.sqrt(jnp.concatenate(pivots, axis=1))
        matrix[:, start : start + 8, 0:RANK] = a[:, 0:8] * scale
        inverse[:, start : start + 8, :] = x[:, 0:8] * scale
        if count > 8:
            matrix[:, start + 8 : stop, 0:RANK] = a[:, 8:]
            matrix[:, start + 8 : stop, RANK:] = x[:, 8:]
        elif stop < RANK:
            lane = lax.broadcasted_iota(jnp.int32, (32, RANK), 1)
            for j in range(3):
                panel = jnp.where(lane >= stop, matrix[j, first:stop, 0:RANK], 0.0)
                both = jnp.concatenate([panel, inverse[j, first:stop, :]], axis=1)
                matrix[j, stop:] = matrix[j, stop:] - tn_dot(panel, both, HIGHEST)[stop:]
        else:
            for j in range(3):
                high, low = split(inverse[j])
                inverse_terms[j, 0:RANK] = high
                inverse_terms[j, RANK:] = low

    def basis_all():
        for j in range(3):
            basis[j][...] = nt_dot(left_in[j][...], inverse[j], HIGHEST)

    def run(name, value):
        parts = range(3 * value, 3 * value + 3)
        if name == "left":
            held["left", value] = left_partial(value)
        elif name == "gram":
            if value == 0:
                for j in range(3):
                    finish(j)
                    gram_partial(j)
                held["gram"] = gram_scatter()
            elif value == 1:
                sent = (gram.at[core, coord[0]], gram_sum.at[0])
                held["gram"] = gram_exchange(held["gram"], (gram_in1, coord[0]), gram_in2, sent, 1, 5)
            elif value == 2:
                sent = (gram_sum.at[0], gram_sum.at[1])
                held["gram"] = gram_exchange(held["gram"], (gram_in2, coord[1]), gram_in3, sent, 2, 8)
            elif value == 3:
                held["gram"] = gram_gather(held["gram"])
            elif value == 4:
                held["gram"] = gram_swap(held["gram"])
            else:
                gram_finish(held["gram"])
        elif name == "chol":
            for piece in range(2 * value, 2 * value + 2):
                eliminate(piece)
            if value == 7:
                basis_all()
        elif name == "norms":
            (swap_norms, finish_norms)[value]()
        elif name == "sent":
            for load in weight_loads:
                load.wait()
            for copy in started:
                copy.wait_send()
            started.clear()
            for k in range(N_PARTS):
                wait_all(partial[k].at[0:60], send_sem.at[k, 0])
                wait_all(pairs[k], send_sem.at[k, 2])
                wait_all(pairs[k], send_sem.at[k, 3])
            wait_all(norms.at[0:9], norm_send.at[0])
        for k in parts:
            if name == "R1a":
                factor_part(k)
                reduce_start(k, 1)
            elif name == "R1b":
                reduce_relay(k, 1)
            elif name == "R1c":
                reduce_finish(k, 1)
                reduce_start(k, 2)
            elif name == "R2b":
                reduce_relay(k, 2)
            elif name == "R2c":
                reduce_finish(k, 2)
                exchange_start(k)
            elif name == "R3c":
                exchange_middle(k)
            elif name == "G3c":
                exchange_finish(k)
                gather_start(k, 2)
            elif name == "G2b":
                gather_relay(k, 2)
            elif name == "G2c":
                gather_finish(k, 2)
                apply_inverse(k)
                gather_start(k, 1)
            elif name == "G1b":
                gather_relay(k, 1)
            elif name == "G1c":
                gather_finish(k, 1)

    pl.semaphore_wait(barrier, len(peers))
    for name, value in PLAN:
        run(name, value)
    for copy in started:
        copy.wait_send()
    for k in range(N_PARTS):
        wait_all(partial[k].at[0:60], send_sem.at[k, 1])


def update_kernel(
    weight_in,
    factor,
    buffer,
    rows_in,
    squares,
    moment_out,
    weight_out,
    right_out,
    change_out,
    moment_box,
    weight_box,
    right_box,
    change_box,
    store_sem,
):
    scale = 1.0 / (jnp.sqrt(squares[...]) + EPSILON)
    where = {unit: (k, slot) for k, part in enumerate(PARTS) for slot, unit in enumerate(part)}
    for j, units in GROUPS:
        rows, pad = ROWS[j], PADDED[j]
        for unit in units:
            k, slot = where[j, unit]
            start = unit * UNIT
            width = min(UNIT, COLS[j] - start)
            value = factor[k][0 : width // 8, slot * 8 : slot * 8 + 8, :].reshape(width, RANK)
            cols = slice(start, start + width)
            right_box[j][cols, :] = value * scale[j : j + 1]
            high, low = split(value)
            product = nt_dot(rows_in[j][...], jnp.concatenate([high, low], axis=1))
            change = product[0:rows] + product[pad : pad + rows]
            change_box[j][:, cols] = change
            moment_box[j][:, cols] = buffer[j][:, cols] - product[2 * pad : 2 * pad + rows]
            weight_box[j][:, cols] = (weight_in[j][:, cols].astype(F32) - change).astype(BF16)
        cols = slice(units[0] * UNIT, min(units[-1] * UNIT + UNIT, COLS[j]))
        pltpu.make_async_copy(right_box[j].at[cols, :], right_out[j].at[cols, :], store_sem.at[j, 0]).start()
        for n, (box, out) in enumerate(((change_box, change_out), (moment_box, moment_out), (weight_box, weight_out))):
            pltpu.make_async_copy(box[j].at[:, cols], out[j].at[:, cols], store_sem.at[j, n + 1]).start()
    for j in range(3):
        for n, (box, out) in enumerate(
            ((right_box, right_out), (change_box, change_out), (moment_box, moment_out), (weight_box, weight_out))
        ):
            pltpu.make_async_copy(box[j], out[j], store_sem.at[j, n]).wait()


def local(
    out_momentum,
    out_gradient,
    out_weight,
    out_right,
    up_momentum,
    up_gradient,
    up_weight,
    up_right,
    down_momentum,
    down_gradient,
    down_weight,
    down_right,
):
    momentum = [down_momentum, out_momentum, up_momentum]
    gradient = [down_gradient, out_gradient, up_gradient]
    weight = [down_weight, out_weight, up_weight]
    right = [down_right, out_right, up_right]
    vmem = pltpu.VMEM
    anywhere = pl.BlockSpec(memory_space=pl.ANY)
    inside = pl.BlockSpec(memory_space=vmem)
    dma = pltpu.SemaphoreType.DMA
    each_part = lambda lead: [vmem((*lead, HEIGHT[k], RANK), F32) for k in range(N_PARTS)]

    factor_shapes = [jax.ShapeDtypeStruct((64, HEIGHT[k], RANK), F32) for k in range(N_PARTS)]
    buffer_shapes = [jax.ShapeDtypeStruct((ROWS[j], COLS[j]), F32) for j in range(3)]
    rows_shapes = [jax.ShapeDtypeStruct((3 * PADDED[j], 2 * RANK), BF16) for j in range(3)]
    weight_shapes = [jax.ShapeDtypeStruct((ROWS[j], COLS[j]), BF16) for j in range(3)]
    middle = [factor_shapes, buffer_shapes, rows_shapes, jax.ShapeDtypeStruct((8, RANK), F32), weight_shapes]
    placed = jax.tree.map(lambda s: vmem(s.shape, s.dtype), middle)
    terms_cols = [UNIT * count for count in UNITS]
    middle = pl.pallas_call(
        reduce_kernel,
        out_shape=placed,
        in_specs=[[anywhere] * 3] * 4,
        out_specs=jax.tree.map(lambda s: inside, middle),
        scratch_shapes=[
            each_part((64,)),
            each_part((16,)),
            each_part((6, 8)),
            each_part((6, 2)),
            each_part((2, 4)),
            each_part((4,)),
            [vmem((ROWS[j], COLS[j]), BF16) for j in range(3)],
            [vmem((COLS[j], RANK), F32) for j in range(3)],
            [vmem((3 * PADDED[j], terms_cols[j]), BF16) for j in range(3)],
            [vmem((PADDED[j], RANK), F32) for j in range(3)],
            [vmem((PADDED[j], RANK), F32) for j in range(3)],
            [vmem((RANK, TERMS[j]), BF16) for j in range(3)],
            vmem((2, 4, 3, 16, RANK), F32),
            vmem((4, 3, 16, RANK), F32),
            vmem((4, 3, 16, RANK), F32),
            vmem((4, 3, 16, RANK), F32),
            vmem((2, 3, 16, RANK), F32),
            vmem((2, 4, 3, 16, RANK), F32),
            vmem((3, RANK, 2 * RANK), F32),
            vmem((3, RANK, RANK), F32),
            vmem((3, 2 * RANK, RANK), BF16),
            [vmem((PADDED[j], RANK), F32) for j in range(3)],
            vmem((12, 8, RANK), F32),
            vmem((2, 8, RANK), F32),
            dma((3, 4, 3)),
            dma((N_PARTS, 4)),
            dma((N_PARTS, 14)),
            dma((17,)),
            dma((17,)),
            dma((1,)),
            dma((3,)),
        ],
        compiler_params=pltpu.CompilerParams(
            collective_id=0, has_side_effects=True, vmem_limit_bytes=45 * 2**20
        ),
        name="reduce",
    )(momentum, gradient, right, weight)
    keep = lambda x: pltpu.with_memory_space_constraint(x, vmem)
    factor, buffer, rows_in, squares, weight = jax.tree.map(keep, tuple(middle))
    matrices = lambda dtype: [jax.ShapeDtypeStruct((ROWS[j], COLS[j]), dtype) for j in range(3)]
    factors = [jax.ShapeDtypeStruct((COLS[j], RANK), F32) for j in range(3)]
    results = [matrices(F32), matrices(BF16), factors, matrices(F32)]
    moment, weight, right, change = pl.pallas_call(
        update_kernel,
        out_shape=results,
        in_specs=[[inside] * 3, [inside] * N_PARTS, [inside] * 3, [inside] * 3, inside],
        out_specs=jax.tree.map(lambda s: anywhere, results),
        scratch_shapes=[
            [vmem((ROWS[j], COLS[j]), F32) for j in range(3)],
            [vmem((ROWS[j], COLS[j]), BF16) for j in range(3)],
            [vmem((COLS[j], RANK), F32) for j in range(3)],
            [vmem((ROWS[j], COLS[j]), F32) for j in range(3)],
            dma((3, 4)),
        ],
        compiler_params=pltpu.CompilerParams(vmem_limit_bytes=40 * 2**20),
        name="update",
    )(weight, factor, buffer, rows_in, squares)
    pick = lambda group: (group[1], group[2], group[0])
    return (*pick(moment), *pick(weight), *pick(right), *pick(change))


def solution(mesh):
    matrix, factor = P(("fsdp", "rep"), "tp"), P("tp", None)
    in_specs = (matrix, matrix, matrix, factor) * 3
    out_specs = (matrix,) * 6 + (factor,) * 3 + (matrix,) * 3
    return jax.shard_map(local, mesh=mesh, in_specs=in_specs, out_specs=out_specs, check_vma=False)
```

```python
import functools
import math

import jax
import jax.numpy as jnp
from jax import lax
from jax.experimental import pallas as pl
from jax.experimental.pallas import tpu as pltpu
from jax.sharding import PartitionSpec as P

ROWS = (216, 80, 80)
PADDED = (224, 80, 80)
COLS = (2560, 2560, 6912)
UNITS = (5, 5, 14)
SPANS = ((1280, 1280), (1280, 1280), (2304, 2304, 2304))
SHAPE = ((13824, 5120), (5120, 5120), (5120, 13824))
UNIT = 512
RANK = 128
DECAY = 0.95
LEARN_RATE = 0.02
EPSILON = 1e-08
MESH = pl.DeviceIdType.MESH
F32 = jnp.float32
BF16 = jnp.bfloat16
HIGHEST = lax.Precision.HIGHEST
AXES = ((0, 1, 2), (1, 2, 0), (2, 0, 1))
TERMS = tuple(3 * rows + (-3 * rows) % 128 for rows in PADDED)

PER_PART = ((3, 3, 3), (3, 3, 3), (2, 2, 2))


def make_parts():
    units = [(matrix, unit) for matrix in range(3) for unit in range(UNITS[matrix])]
    parts = []
    for count in sum(PER_PART, ()):
        parts.append(units[:count])
        units = units[count:]
    return parts


PARTS = make_parts()
N_PARTS = len(PARTS)
GROUPS = ((1, (0, 1)), (1, (2, 3)), (1, (4,)), (0, (0, 1)), (0, (2, 3)), (0, (4,))) + tuple(
    (2, (unit, unit + 1)) for unit in range(0, 14, 2)
)
PLAN = (
    ("left", 0),
    ("left", 1),
    ("R1a", 0),
    ("left", 2),
    ("R1b", 0),
    ("gram", 0),
    ("R1a", 1),
    ("gram", 1),
    ("R1c", 0),
    ("R1b", 1),
    ("R1a", 2),
    ("gram", 2),
    ("R2b", 0),
    ("R1c", 1),
    ("R1b", 2),
    ("gram", 3),
    ("R2c", 0),
    ("R2b", 1),
    ("R1c", 2),
    ("R3c", 0),
    ("gram", 4),
    ("R2c", 1),
    ("gram", 5),
    ("chol", 0),
    ("R2b", 2),
    ("chol", 1),
    ("G3c", 0),
    ("chol", 2),
    ("R3c", 1),
    ("chol", 3),
    ("R2c", 2),
    ("chol", 4),
    ("G2b", 0),
    ("chol", 5),
    ("chol", 6),
    ("G3c", 1),
    ("chol", 7),
    ("R3c", 2),
    ("G2c", 0),
    ("G2b", 1),
    ("G3c", 2),
    ("G1b", 0),
    ("G2b", 2),
    ("G2c", 1),
    ("G2c", 2),
    ("G1b", 1),
    ("G1c", 0),
    ("G1b", 2),
    ("norms", 0),
    ("sent", 0),
    ("G1c", 1),
    ("norms", 1),
    ("G1c", 2),
)
HEIGHT = [8 * len(part) for part in PARTS]


def split(value):
    high = value.astype(BF16)
    return high, (value - high.astype(F32)).astype(BF16)


def nt_dot(first, second, precision=None):
    return lax.dot_general(first, second, (((1,), (1,)), ((), ())), precision=precision, preferred_element_type=F32)


def tn_dot(first, second, precision=None):
    return lax.dot_general(first, second, (((0,), (0,)), ((), ())), precision=precision, preferred_element_type=F32)


def each(count, body):
    def step(index, carry):
        body(index)
        return carry

    lax.fori_loop(0, count, step, 0)


def reduce_kernel(
    momentum,
    gradient,
    right,
    weight,
    factor,
    buffer,
    rows_out,
    squares,
    weight_in,
    partial,
    summed,
    inbox1,
    inbox2,
    inbox3,
    pairs,
    grad_in,
    right_in,
    terms,
    left,
    left_in,
    left_terms,
    gram,
    gram_in1,
    gram_in2,
    gram_in3,
    gram_sum,
    gram_all,
    matrix,
    inverse,
    inverse_terms,
    basis,
    norms,
    squares_in,
    load_sem,
    send_sem,
    recv_sem,
    misc_send,
    misc_recv,
    norm_send,
    norm_recv,
):
    rows_at = lax.axis_index("fsdp")
    core = lax.axis_index("tp")
    coord = (lax.axis_index("rep"), rows_at % 4, rows_at // 4)

    def device(axis, shift):
        moved = [(coord[a] + shift) % 4 if a == axis else coord[a] for a in range(3)]
        return (moved[2] * 4 + moved[1], core, moved[0])

    partner = (rows_at, 1 - core, coord[0])

    loads = []
    for j in range(3):
        steps = []
        start = 0
        for s, span in enumerate(SPANS[j]):
            cols = pl.ds(start, span)
            copies = [
                pltpu.make_async_copy(momentum[j].at[:, cols], buffer[j].at[:, cols], load_sem.at[j, s, 0]),
                pltpu.make_async_copy(gradient[j].at[:, cols], grad_in[j].at[:, cols], load_sem.at[j, s, 1]),
                pltpu.make_async_copy(right[j].at[cols, :], right_in[j].at[cols, :], load_sem.at[j, s, 2]),
            ]
            for copy in copies:
                copy.start()
            steps.append((start, span, copies))
            start += span
        loads.append(steps)

    weight_loads = [pltpu.make_async_copy(weight[j], weight_in[j], load_sem.at[j, 3, 0]) for j in range(3)]
    for copy in weight_loads:
        copy.start()

    barrier = pltpu.get_barrier_semaphore()
    peers = [device(axis, shift) for axis in range(3) for shift in (1, 2, 3)] + [partner]
    for peer in peers:
        pl.semaphore_signal(barrier, inc=1, device_id=peer, device_id_type=MESH)

    started = []

    def send(first, second, src, dst, target):
        copy = pltpu.make_async_remote_copy(
            src_ref=src, dst_ref=dst, send_sem=first, recv_sem=second, device_id=target, device_id_type=MESH
        )
        copy.start()
        return copy

    def misc(index, src, dst, target):
        copy = send(misc_send.at[index], misc_recv.at[index], src, dst, target)
        started.append(copy)
        return copy

    def wait_all(ref, sem):
        pltpu.make_async_copy(ref, ref, sem).wait()

    held = {}

    def left_partial(j):
        pad = PADDED[j]
        total = None
        for start, span, copies in loads[j]:
            for copy in copies:
                copy.wait()

            def prepare(i, start=start):
                cols = pl.ds(pl.multiple_of(start + i * 256, 256), 256)
                value = buffer[j][:, cols] + grad_in[j][:, cols].astype(F32)
                buffer[j][:, cols] = value
                if pad > ROWS[j]:
                    value = jnp.concatenate([value, jnp.zeros((pad - ROWS[j], 256), F32)], axis=0)
                high, low = split(value)
                terms[j][0:pad, cols] = high
                terms[j][pad : 2 * pad, cols] = low
                terms[j][2 * pad : 3 * pad, cols] = high

            each(span // 256, prepare)
            right_terms = jnp.concatenate(split(right_in[j][start : start + span, :]), axis=1)
            product = jnp.dot(terms[j][0 : 2 * pad, start : start + span], right_terms, preferred_element_type=F32)
            product = product[0:pad, 0:RANK] + (product[0:pad, RANK:] + product[pad:, 0:RANK])
            total = product if total is None else total + product
        left[j][...] = total
        if terms[j].shape[1] > COLS[j]:
            terms[j][:, COLS[j] :] = jnp.zeros((3 * pad, terms[j].shape[1] - COLS[j]), BF16)
        if j == 0:
            pl.semaphore_wait(barrier, len(peers))
        return misc(j, left[j], left_in[j], partner)

    def left_finish(j, copy):
        copy.wait_recv()
        pad = PADDED[j]
        value = left[j][...] + left_in[j][...]
        left_in[j][...] = value
        high = value.astype(BF16).astype(F32)
        low = value - high
        pieces = [high, high, low]
        if TERMS[j] > 3 * pad:
            pieces.append(jnp.zeros((TERMS[j] - 3 * pad, RANK), F32))
        left_terms[j][...] = jnp.concatenate(pieces, axis=0).T.astype(BF16)

    def gram_partial(j):
        value = left_in[j][...]
        result = tn_dot(value, value, HIGHEST)
        gram[:, :, j] = result.reshape(2, 4, 16, RANK)

    def factor_unit(k, slot):
        j, unit = PARTS[k][slot]
        cols = slice(unit * UNIT, (unit + 1) * UNIT)
        product = jnp.dot(left_terms[j][:, 0 : 3 * PADDED[j]], terms[j][:, cols], preferred_element_type=F32)
        partial[k][:, slot * 8 : slot * 8 + 8, :] = product.T.reshape(64, 8, RANK)

    finished = set()

    def finish(j):
        if j not in finished:
            finished.add(j)
            left_finish(j, held["left", j])

    def factor_part(k):
        for j in sorted({j for j, _ in PARTS[k]}):
            finish(j)
        for slot in range(len(PARTS[k])):
            factor_unit(k, slot)

    def place(ref, base, half, chunk, side):
        return ref.at[pl.ds(base + ((chunk % 4) * 2 + side) * half, half)]

    def first_coord(k):
        return coord[AXES[k % 3][0]]

    def reduce_setting(k, phase):
        axis = AXES[k % 3][phase - 1]
        base, half, inbox = (0, 8, inbox1[k]) if phase == 1 else (16 * first_coord(k), 2, inbox2[k])
        at = functools.partial(place, partial[k], base, half)

        def out(n, ref, box, shift):
            sem = recv_sem.at[k, 3 * (phase - 1) + min(n, 2)]
            send(send_sem.at[k, 0], sem, ref, inbox.at[box], device(axis, shift))

        return coord[axis], at, half, inbox, out

    def reduce_start(k, phase):
        i, at, half, inbox, out = reduce_setting(k, phase)
        out(0, at(i + 2, 0), 0, 1)
        out(1, at(i + 2, 1), 1, 3)
        out(2, at(i + 1, 1), 2, 1)
        out(2, at(i + 3, 0), 3, 3)

    def reduce_relay(k, phase):
        i, at, half, inbox, out = reduce_setting(k, phase)
        for side, chunk, shift in ((0, i + 1, 1), (1, i + 3, 3)):
            wait_all(inbox.at[side], recv_sem.at[k, 3 * (phase - 1) + side])
            ref = at(chunk, side)
            ref[...] += inbox[side]
            out(2, ref, 4 + side, shift)

    def reduce_finish(k, phase):
        i, at, half, inbox, out = reduce_setting(k, phase)
        wait_all(inbox.at[2:6], recv_sem.at[k, 3 * (phase - 1) + 2])
        for side, near, relayed in ((0, 3, 4), (1, 2, 5)):
            at(i, side)[...] += inbox[near] + inbox[relayed]

    def exchange_setting(k):
        axes = AXES[k % 3]
        second, third = coord[axes[1]], coord[axes[2]]
        shifts = (1 + 2 * (third % 2), 3 - 2 * (third % 2))
        return axes[2], shifts, pl.ds(16 * coord[axes[0]] + 4 * second, 4), pl.ds(4 * second, 4)

    def exchange_start(k):
        axis, shifts, mine, _ = exchange_setting(k)
        send(send_sem.at[k, 2], recv_sem.at[k, 6], partial[k].at[mine], inbox3[k].at[0], device(axis, shifts[0]))

    def exchange_middle(k):
        axis, shifts, mine, _ = exchange_setting(k)
        wait_all(inbox3[k].at[0], recv_sem.at[k, 6])
        pairs[k][...] = partial[k][mine] + inbox3[k][0]
        send(send_sem.at[k, 3], recv_sem.at[k, 7], pairs[k], inbox3[k].at[1], device(axis, shifts[1]))

    def exchange_finish(k):
        _, _, _, there = exchange_setting(k)
        wait_all(inbox3[k].at[1], recv_sem.at[k, 7])
        summed[k][there] = pairs[k][...] + inbox3[k][1]

    def gather_setting(k, phase):
        axis = AXES[k % 3][phase - 1]
        ref, half, first = (factor[k], 8, 11) if phase == 1 else (summed[k], 2, 8)
        at = functools.partial(place, ref, 0, half)

        def out(n, there, shift):
            send(send_sem.at[k, 1], recv_sem.at[k, first + n], there, there, device(axis, shift))

        def arrived(n):
            wait_all(ref.at[0:half] if n < 2 else ref.at[0 : 4 * half], recv_sem.at[k, first + n])

        return coord[axis], at, out, arrived

    def gather_start(k, phase):
        i, at, out, arrived = gather_setting(k, phase)
        out(0, at(i, 0), 1)
        out(1, at(i, 1), 3)
        out(2, at(i, 1), 1)
        out(2, at(i, 0), 3)

    def gather_relay(k, phase):
        i, at, out, arrived = gather_setting(k, phase)
        arrived(0)
        out(2, at(i + 3, 0), 1)
        arrived(1)
        out(2, at(i + 1, 1), 3)

    def gather_finish(k, phase):
        gather_setting(k, phase)[3](2)

    sums = [[jnp.zeros((8, RANK), F32) for _ in range(3)] for _ in range(3)]
    counted = [0] * 3

    def send_norms(part):
        axis = AXES[part][0]
        rows = [jnp.sum(value, axis=0, keepdims=True) for value in sums[part]]
        ref = norms.at[4 * part + coord[axis]]
        ref[...] = jnp.concatenate(rows + [jnp.zeros((5, RANK), F32)], axis=0)
        for shift in (1, 2, 3):
            send(norm_send.at[0], norm_recv.at[part], ref, ref, device(axis, shift))

    def swap_norms():
        total = None
        for part in range(3):
            wait_all(norms.at[0:3], norm_recv.at[part])
            n = 4 * part
            value = (norms[n] + norms[n + 1]) + (norms[n + 2] + norms[n + 3])
            total = value if total is None else total + value
        squares_in[0] = total
        held["norms"] = misc(16, squares_in.at[0], squares_in.at[1], partner)

    def finish_norms():
        held["norms"].wait_recv()
        total = squares_in[0] + squares_in[1]
        squares[...] = total
        scale = 1.0 / (jnp.sqrt(total) + EPSILON)
        for j in range(3):
            pad = PADDED[j]
            value = basis[j][...]
            step_size = LEARN_RATE * math.sqrt(SHAPE[j][0] / SHAPE[j][1])
            high, low = split(value * (scale[j : j + 1] * step_size))
            rows_out[j][0:pad, 0:RANK] = high
            rows_out[j][0:pad, RANK:] = high
            rows_out[j][pad : 2 * pad, 0:RANK] = low
            rows_out[j][pad : 2 * pad, RANK:] = jnp.zeros((pad, RANK), BF16)
            rows_out[j][2 * pad :, 0:RANK] = (value * (1.0 - DECAY)).astype(BF16)
            rows_out[j][2 * pad :, RANK:] = jnp.zeros((pad, RANK), BF16)

    def apply_inverse(k):
        base = 16 * first_coord(k)
        for j in range(3):
            slots = [slot for slot, (other, _) in enumerate(PARTS[k]) if other == j]
            if not slots:
                continue
            rows = slice(slots[0] * 8, slots[-1] * 8 + 8)
            count = 8 * len(slots)
            high, low = split(summed[k][:, rows, :].reshape(16 * count, RANK))
            product = nt_dot(jnp.concatenate([high, low], axis=0), inverse_terms[j])
            product = product[: 16 * count, :RANK] + (product[: 16 * count, RANK:] + product[16 * count :, :RANK])
            factor[k][pl.ds(base, 16), rows, :] = product.reshape(16, count, RANK)
            total = jnp.sum((product * product).reshape(2 * count, 8, RANK), axis=0)
            sums[k % 3][j] = sums[k % 3][j] + total
        counted[k % 3] += 1
        if counted[k % 3] == N_PARTS // 3:
            send_norms(k % 3)

    def gram_scatter():
        x = coord[0]
        return [
            misc(2 + s, gram.at[core, (x + s) % 4], gram_in1.at[x], device(0, s)) for s in (1, 2, 3)
        ]

    def gram_exchange(copies, own_value, box, sent, axis, n):
        for copy in copies:
            copy.wait_recv()
        box_before, at_before = own_value
        box_before[at_before] = sent[0][...]
        sent[1][...] = (box_before[0] + box_before[1]) + (box_before[2] + box_before[3])
        return [misc(n + s, sent[1], box.at[coord[axis]], device(axis, s)) for s in (1, 2, 3)]

    def gram_gather(copies):
        x = coord[0]
        for copy in copies:
            copy.wait_recv()
        gram_in3[coord[2]] = gram_sum[1]
        ref = gram_all.at[core, x]
        ref[...] = (gram_in3[0] + gram_in3[1]) + (gram_in3[2] + gram_in3[3])
        return [misc(11 + s, ref, ref, device(0, s)) for s in (1, 2, 3)]

    def gram_swap(copies):
        for copy in copies:
            copy.wait_recv()
        return misc(15, gram_all.at[core], gram_all.at[core], partner)

    def gram_finish(copy):
        copy.wait_recv()
        row = lax.broadcasted_iota(jnp.int32, (RANK, RANK), 0)
        col = lax.broadcasted_iota(jnp.int32, (RANK, RANK), 1)
        for j in range(3):
            matrix[j, :, 0:RANK] = gram_all[:, :, j].reshape(RANK, RANK)
            matrix[j, :, RANK:] = (row == col).astype(F32)

    def eliminate(piece):
        first, start = piece // 4 * 32, piece * 8
        stop = first + 32
        count = stop - start
        a = matrix[:, start:stop, 0:RANK]
        x = matrix[:, start:stop, RANK:]
        rows = lax.broadcasted_iota(jnp.int32, (3, count, RANK), 1)
        columns = [jnp.broadcast_to(a[:, :, start + n : start + n + 1], (3, count, RANK)) for n in range(8)]
        pivots = []
        for n in range(8):
            pivot = columns[n][:, n : n + 1, :]
            pivots.append(pivot)
            scale = 1.0 / jnp.broadcast_to(pivot, (3, 8, RANK))
            ratio = jnp.where(rows > n, columns[n] * scale[:, 0:1, :], 0.0)
            for later in range(n + 1, 8):
                columns[later] = columns[later] - ratio * columns[later][:, n : n + 1, :]
            a = a - ratio * a[:, n : n + 1, :]
            x = x - ratio * x[:, n : n + 1, :]
        scale = 1.0 / jnp.sqrt(jnp.concatenate(pivots, axis=1))
        matrix[:, start : start + 8, 0:RANK] = a[:, 0:8] * scale
        inverse[:, start : start + 8, :] = x[:, 0:8] * scale
        if count > 8:
            matrix[:, start + 8 : stop, 0:RANK] = a[:, 8:]
            matrix[:, start + 8 : stop, RANK:] = x[:, 8:]
        elif stop < RANK:
            lane = lax.broadcasted_iota(jnp.int32, (32, RANK), 1)
            for j in range(3):
                panel = jnp.where(lane >= stop, matrix[j, first:stop, 0:RANK], 0.0)
                both = jnp.concatenate([panel, inverse[j, first:stop, :]], axis=1)
                matrix[j, stop:] = matrix[j, stop:] - tn_dot(panel, both, HIGHEST)[stop:]
        else:
            for j in range(3):
                high, low = split(inverse[j])
                inverse_terms[j, 0:RANK] = high
                inverse_terms[j, RANK:] = low

    def basis_all():
        for j in range(3):
            basis[j][...] = nt_dot(left_in[j][...], inverse[j], HIGHEST)

    def run(name, value):
        parts = range(3 * value, 3 * value + 3)
        if name == "left":
            held["left", value] = left_partial(value)
        elif name == "gram":
            if value == 0:
                for j in range(3):
                    finish(j)
                    gram_partial(j)
                held["gram"] = gram_scatter()
            elif value == 1:
                sent = (gram.at[core, coord[0]], gram_sum.at[0])
                held["gram"] = gram_exchange(held["gram"], (gram_in1, coord[0]), gram_in2, sent, 1, 5)
            elif value == 2:
                sent = (gram_sum.at[0], gram_sum.at[1])
                held["gram"] = gram_exchange(held["gram"], (gram_in2, coord[1]), gram_in3, sent, 2, 8)
            elif value == 3:
                held["gram"] = gram_gather(held["gram"])
            elif value == 4:
                held["gram"] = gram_swap(held["gram"])
            else:
                gram_finish(held["gram"])
        elif name == "chol":
            for piece in range(2 * value, 2 * value + 2):
                eliminate(piece)
            if value == 7:
                basis_all()
        elif name == "norms":
            (swap_norms, finish_norms)[value]()
        elif name == "sent":
            for load in weight_loads:
                load.wait()
            for copy in started:
                copy.wait_send()
            started.clear()
            for k in range(N_PARTS):
                wait_all(partial[k].at[0:60], send_sem.at[k, 0])
                wait_all(pairs[k], send_sem.at[k, 2])
                wait_all(pairs[k], send_sem.at[k, 3])
            wait_all(norms.at[0:9], norm_send.at[0])
        for k in parts:
            if name == "R1a":
                factor_part(k)
                reduce_start(k, 1)
            elif name == "R1b":
                reduce_relay(k, 1)
            elif name == "R1c":
                reduce_finish(k, 1)
                reduce_start(k, 2)
            elif name == "R2b":
                reduce_relay(k, 2)
            elif name == "R2c":
                reduce_finish(k, 2)
                exchange_start(k)
            elif name == "R3c":
                exchange_middle(k)
            elif name == "G3c":
                exchange_finish(k)
                gather_start(k, 2)
            elif name == "G2b":
                gather_relay(k, 2)
            elif name == "G2c":
                gather_finish(k, 2)
                apply_inverse(k)
                gather_start(k, 1)
            elif name == "G1b":
                gather_relay(k, 1)
            elif name == "G1c":
                gather_finish(k, 1)

    for name, value in PLAN:
        run(name, value)
    for copy in started:
        copy.wait_send()
    for k in range(N_PARTS):
        wait_all(partial[k].at[0:60], send_sem.at[k, 1])


def update_kernel(
    weight_in,
    factor,
    buffer,
    rows_in,
    squares,
    moment_out,
    weight_out,
    right_out,
    change_out,
    moment_box,
    weight_box,
    right_box,
    change_box,
    store_sem,
):
    scale = 1.0 / (jnp.sqrt(squares[...]) + EPSILON)
    where = {unit: (k, slot) for k, part in enumerate(PARTS) for slot, unit in enumerate(part)}
    for j, units in GROUPS:
        rows, pad = ROWS[j], PADDED[j]
        for unit in units:
            k, slot = where[j, unit]
            start = unit * UNIT
            width = min(UNIT, COLS[j] - start)
            value = factor[k][0 : width // 8, slot * 8 : slot * 8 + 8, :].reshape(width, RANK)
            cols = slice(start, start + width)
            right_box[j][cols, :] = value * scale[j : j + 1]
            high, low = split(value)
            product = nt_dot(rows_in[j][...], jnp.concatenate([high, low], axis=1))
            change = product[0:rows] + product[pad : pad + rows]
            change_box[j][:, cols] = change
            moment_box[j][:, cols] = buffer[j][:, cols] - product[2 * pad : 2 * pad + rows]
            weight_box[j][:, cols] = (weight_in[j][:, cols].astype(F32) - change).astype(BF16)
        cols = slice(units[0] * UNIT, min(units[-1] * UNIT + UNIT, COLS[j]))
        pltpu.make_async_copy(right_box[j].at[cols, :], right_out[j].at[cols, :], store_sem.at[j, 0]).start()
        for n, (box, out) in enumerate(((change_box, change_out), (moment_box, moment_out), (weight_box, weight_out))):
            pltpu.make_async_copy(box[j].at[:, cols], out[j].at[:, cols], store_sem.at[j, n + 1]).start()
    for j in range(3):
        for n, (box, out) in enumerate(
            ((right_box, right_out), (change_box, change_out), (moment_box, moment_out), (weight_box, weight_out))
        ):
            pltpu.make_async_copy(box[j], out[j], store_sem.at[j, n]).wait()


def local(
    out_momentum,
    out_gradient,
    out_weight,
    out_right,
    up_momentum,
    up_gradient,
    up_weight,
    up_right,
    down_momentum,
    down_gradient,
    down_weight,
    down_right,
):
    momentum = [down_momentum, out_momentum, up_momentum]
    gradient = [down_gradient, out_gradient, up_gradient]
    weight = [down_weight, out_weight, up_weight]
    right = [down_right, out_right, up_right]
    vmem = pltpu.VMEM
    anywhere = pl.BlockSpec(memory_space=pl.ANY)
    inside = pl.BlockSpec(memory_space=vmem)
    dma = pltpu.SemaphoreType.DMA
    each_part = lambda lead: [vmem((*lead, HEIGHT[k], RANK), F32) for k in range(N_PARTS)]

    factor_shapes = [jax.ShapeDtypeStruct((64, HEIGHT[k], RANK), F32) for k in range(N_PARTS)]
    buffer_shapes = [jax.ShapeDtypeStruct((ROWS[j], COLS[j]), F32) for j in range(3)]
    rows_shapes = [jax.ShapeDtypeStruct((3 * PADDED[j], 2 * RANK), BF16) for j in range(3)]
    weight_shapes = [jax.ShapeDtypeStruct((ROWS[j], COLS[j]), BF16) for j in range(3)]
    middle = [factor_shapes, buffer_shapes, rows_shapes, jax.ShapeDtypeStruct((8, RANK), F32), weight_shapes]
    placed = jax.tree.map(lambda s: vmem(s.shape, s.dtype), middle)
    terms_cols = [UNIT * count for count in UNITS]
    middle = pl.pallas_call(
        reduce_kernel,
        out_shape=placed,
        in_specs=[[anywhere] * 3] * 4,
        out_specs=jax.tree.map(lambda s: inside, middle),
        scratch_shapes=[
            each_part((64,)),
            each_part((16,)),
            each_part((6, 8)),
            each_part((6, 2)),
            each_part((2, 4)),
            each_part((4,)),
            [vmem((ROWS[j], COLS[j]), BF16) for j in range(3)],
            [vmem((COLS[j], RANK), F32) for j in range(3)],
            [vmem((3 * PADDED[j], terms_cols[j]), BF16) for j in range(3)],
            [vmem((PADDED[j], RANK), F32) for j in range(3)],
            [vmem((PADDED[j], RANK), F32) for j in range(3)],
            [vmem((RANK, TERMS[j]), BF16) for j in range(3)],
            vmem((2, 4, 3, 16, RANK), F32),
            vmem((4, 3, 16, RANK), F32),
            vmem((4, 3, 16, RANK), F32),
            vmem((4, 3, 16, RANK), F32),
            vmem((2, 3, 16, RANK), F32),
            vmem((2, 4, 3, 16, RANK), F32),
            vmem((3, RANK, 2 * RANK), F32),
            vmem((3, RANK, RANK), F32),
            vmem((3, 2 * RANK, RANK), BF16),
            [vmem((PADDED[j], RANK), F32) for j in range(3)],
            vmem((12, 8, RANK), F32),
            vmem((2, 8, RANK), F32),
            dma((3, 4, 3)),
            dma((N_PARTS, 4)),
            dma((N_PARTS, 14)),
            dma((17,)),
            dma((17,)),
            dma((1,)),
            dma((3,)),
        ],
        compiler_params=pltpu.CompilerParams(
            collective_id=0, has_side_effects=True, vmem_limit_bytes=45 * 2**20
        ),
        name="reduce",
    )(momentum, gradient, right, weight)
    keep = lambda x: pltpu.with_memory_space_constraint(x, vmem)
    factor, buffer, rows_in, squares, weight = jax.tree.map(keep, tuple(middle))
    matrices = lambda dtype: [jax.ShapeDtypeStruct((ROWS[j], COLS[j]), dtype) for j in range(3)]
    factors = [jax.ShapeDtypeStruct((COLS[j], RANK), F32) for j in range(3)]
    results = [matrices(F32), matrices(BF16), factors, matrices(F32)]
    moment, weight, right, change = pl.pallas_call(
        update_kernel,
        out_shape=results,
        in_specs=[[inside] * 3, [inside] * N_PARTS, [inside] * 3, [inside] * 3, inside],
        out_specs=jax.tree.map(lambda s: anywhere, results),
        scratch_shapes=[
            [vmem((ROWS[j], COLS[j]), F32) for j in range(3)],
            [vmem((ROWS[j], COLS[j]), BF16) for j in range(3)],
            [vmem((COLS[j], RANK), F32) for j in range(3)],
            [vmem((ROWS[j], COLS[j]), F32) for j in range(3)],
            dma((3, 4)),
        ],
        compiler_params=pltpu.CompilerParams(vmem_limit_bytes=40 * 2**20),
        name="update",
    )(weight, factor, buffer, rows_in, squares)
    pick = lambda group: (group[1], group[2], group[0])
    return (*pick(moment), *pick(weight), *pick(right), *pick(change))


def solution(mesh):
    matrix, factor = P(("fsdp", "rep"), "tp"), P("tp", None)
    in_specs = (matrix, matrix, matrix, factor) * 3
    out_specs = (matrix,) * 6 + (factor,) * 3 + (matrix,) * 3
    return jax.shard_map(local, mesh=mesh, in_specs=in_specs, out_specs=out_specs, check_vma=False)
```
